512 devices in a mesh: blk: 64 (over x, z_lo, y), rep: 8 (over z_hi, core).
Axes of the slice: x: 4, y: 8, z: 8 (z_hi: 4, z_lo: 2; z = z_hi * 2 + z_lo), core: 2. Of those that a mesh axis runs over, the one named last changes fastest.
Arguments:
- features: float32 [24576, 128], P('blk'), may hold values from -6 to 6
- tile_values: float32 [192, 96, 128, 128], P('blk', 'rep'), may hold values from -0.125 to 0.125
- tile_cols: int32 [192, 96], P('blk', 'rep'), may hold values from 0 to 191, as said below
- tile_counts: int32 [192, 8], P('blk', 'rep'), may hold values from 1 to 12, as said below
- degrees: int32 [24576], P('blk'), may hold values from 1 to 2
- curve_order: int32 [24576], P('blk'), may hold values from 0 to 24575, as said below
Outputs:
- hop_tokens: float32 [5, 24576, 128], P(None, 'blk')
The draws below stay inside these ranges and needn't reach their ends.
Inputs may be any that keep to these rules, and one draw needn't show every extreme that they name: With p = i // 3 and w = s // 12, block tile_cols[i, s] lies in cycle position (p - w * 8 - j) mod 64 for some j in 0 to 7, where cycle position q holds blocks q * 3 to (q + 1) * 3 - 1; the 12 slots of one block-row and one w name distinct blocks. tile_counts[i, 0] = 12 for every block-row. `curve_order`: each aligned run of 384 curve positions is a permutation of the node numbers of the same run.
All inputs are finite; a program needn't handle non-finite values.
Results may differ from the reference program's by a relative error of at most 0.00013.
Values sent between devices are 32-bit elements; how exact they have to be, the bound alone decides.
No kernel may reach another device: no remote copies, remote signals or barrier semaphores. Data moves between devices by JAX's collectives and lax.ppermute only.
A program may use at most 64 MiB of HBM per device.

```python
import jax
import jax.numpy as jnp
from jax import lax

D = 128
TILE = 128
HOPS = 4
BLOCKS_DEV = 3
TILES_DEV = 12
CYCLE = 64
GROUPS = 8
SPAN = 8
BLOCKS = 192
SLOTS = 96
NODES = 24576


def first_near(order):
    near_flag = (order < BLOCKS_DEV).astype(jnp.int32)
    place = jnp.argmax(near_flag)
    head = order[0]
    chosen = order[place]
    spots = jnp.arange(order.shape[0], dtype=jnp.int32)
    swapped = jnp.where(spots == place, head, order)
    return jnp.where(spots == 0, chosen, swapped)


def draw_tile_cols(key, part):
    key = jax.random.fold_in(key, 11)
    candidates = SPAN * BLOCKS_DEV
    keys = jax.random.split(key, BLOCKS * GROUPS)
    picks = jax.vmap(lambda k: first_near(jax.random.permutation(k, candidates).astype(jnp.int32))[:TILES_DEV])(keys)
    picks = picks.reshape(BLOCKS, GROUPS, TILES_DEV).astype(jnp.int32)
    offset = picks // BLOCKS_DEV
    within = picks % BLOCKS_DEV
    position = (jnp.arange(BLOCKS, dtype=jnp.int32) // BLOCKS_DEV)[:, None, None]
    group = jnp.arange(GROUPS, dtype=jnp.int32)[None, :, None]
    source = jnp.mod(position - group * SPAN - offset, CYCLE)
    return (source * BLOCKS_DEV + within).reshape(BLOCKS, SLOTS).astype(jnp.int32)


def draw_tile_counts(key, part):
    key = jax.random.fold_in(key, 23)
    others = jax.random.randint(key, (BLOCKS, GROUPS), 1, TILES_DEV + 1, dtype=jnp.int32)
    first = jnp.arange(GROUPS, dtype=jnp.int32)[None, :] == 0
    return jnp.where(first, TILES_DEV, others).astype(jnp.int32)


def draw_curve_order(key, part):
    key = jax.random.fold_in(key, 37)
    run_len = BLOCKS_DEV * TILE
    keys = jax.random.split(key, CYCLE)
    perms = jax.vmap(lambda k: jax.random.permutation(k, run_len))(keys).astype(jnp.int32)
    base = (jnp.arange(CYCLE, dtype=jnp.int32) * run_len)[:, None]
    return (perms + base).reshape(NODES).astype(jnp.int32)


def set_ends(values, stream_key, low, largest):
    index_at = [jax.random.randint(jax.random.fold_in(stream_key, axis), (), 0, length) for axis, length in enumerate(values.shape)]
    main_axis = values.shape.index(max(values.shape))
    neighbour = index_at[:main_axis] + [(index_at[main_axis] + 1) % values.shape[main_axis]] + index_at[main_axis + 1:]
    return values.at[tuple(index_at)].set(low).at[tuple(neighbour)].set(largest)


def level_of(own_key, dims, cuts, low, top_value):
    loudness = 1.0
    for axis_at, blocks in cuts:
        heights = jax.random.uniform(jax.random.fold_in(jax.random.fold_in(own_key, 6), axis_at), (blocks,), jnp.float32, low / len(cuts), top_value / len(cuts))
        loudness = loudness * jnp.repeat(jnp.exp(heights), dims[axis_at] // blocks).reshape((-1,) + (1,) * (len(dims) - 1 - axis_at))
    return loudness


def bell_draw(own_key, shape, scale, most, pieces=(), held_as=jnp.bfloat16):
    gain = level_of(own_key, shape, pieces, -0.22, 0.18) if pieces else 1.0
    values = jax.random.normal(own_key, shape, jnp.float32) * scale * gain
    return jnp.minimum(jnp.maximum(values, -most), most).astype(held_as)


def setup_inputs(seed: int = 0) -> dict:
    streams_of = jax.random.split(jax.random.key(seed), 7)
    return {
        "features": bell_draw(streams_of[0], (NODES, D), 1.0, 6.0, ((0, 64),), jnp.float32),
        "tile_values": bell_draw(streams_of[1], (BLOCKS, SLOTS, TILE, TILE), (SLOTS * 27) ** -0.5, 0.125, ((0, 64), (1, 8)), jnp.float32),
        "tile_cols": draw_tile_cols(jax.random.fold_in(streams_of[6], 71), 0),
        "tile_counts": draw_tile_counts(jax.random.fold_in(streams_of[6], 71), 0),
        "degrees": set_ends(jax.random.randint(streams_of[4], (NODES,), 1, 3), jax.random.fold_in(streams_of[4], 1), 1, 2).astype(jnp.int32),
        "curve_order": draw_curve_order(jax.random.fold_in(streams_of[6], 71), 0),
    }


def reference(features, tile_values, tile_cols, tile_counts, degrees, curve_order):
    current = jnp.take(features, curve_order, axis=0)
    inv_root = lax.rsqrt(degrees.astype(jnp.float32))
    slot_group = jnp.repeat(tile_counts, TILES_DEV, axis=1)
    slot_rank = jnp.arange(SLOTS) % TILES_DEV
    live_mask = (slot_rank[None, :] < slot_group).astype(jnp.float32)
    tokens = [current]
    for hop_number in range(HOPS):
        sent = (inv_root[:, None] * current).reshape(BLOCKS, TILE, D)

        def one_row(parts):
            tiles, cols, weights = parts
            gathered = jnp.take(sent, cols, axis=0) * weights[:, None, None]
            return jnp.einsum('sab,sbc->ac', tiles, gathered, precision=lax.Precision.HIGHEST)
        summed = lax.map(one_row, (tile_values, tile_cols, live_mask))
        current = inv_root[:, None] * summed.reshape(NODES, D)
        tokens.append(current)
    return jnp.stack(tokens)
```

```python
import functools

import jax
import jax.numpy as jnp
from jax import lax
from jax.experimental import pallas as pl
from jax.experimental.pallas import tpu as pltpu
from jax.sharding import PartitionSpec as P

HOPS = 4
CHAINS = 2
HALF = 64


def send(block, place):
    cycle, groups = lax.axis_size("blk"), lax.axis_size("rep")
    route = []
    for p in range(cycle):
        for w in range(groups):
            to_p, to_w = place(p, w)
            route.append((p * groups + w, (to_p % cycle) * groups + to_w))
    return lax.ppermute(block, ("blk", "rep"), route)


def ahead(block, distance):
    return send(block, lambda p, w: (p + distance, w))


def pack(field, chain):
    blocks = field.shape[0] // 128
    half = field.reshape(blocks, 2, HALF, 2, HALF)[:, :, :, chain]
    return half.transpose(0, 2, 1, 3).reshape(blocks * HALF, 128)


def split_tiles(tiles_ref, out_ref):
    for s in range(tiles_ref.shape[1]):
        tile = tiles_ref[0, s]
        high = tile.astype(jnp.bfloat16)
        low = (tile - high.astype(jnp.float32)).astype(jnp.bfloat16)
        out_ref[0, 0:128, s * 128:(s + 1) * 128] = high
        out_ref[0, 128:256, s * 128:(s + 1) * 128] = low


def tile_parts(tile_values):
    rows, slots = tile_values.shape[:2]
    return pl.pallas_call(
        split_tiles,
        grid=(rows,),
        in_specs=[pl.BlockSpec((1, slots, 128, 128), lambda i: (i, 0, 0, 0))],
        out_specs=pl.BlockSpec((1, 256, slots * 128), lambda i: (i, 0, 0)),
        out_shape=jax.ShapeDtypeStruct((rows, 256, slots * 128), jnp.bfloat16),
        compiler_params=pltpu.CompilerParams(vmem_limit_bytes=32 * 2**20),
    )(tile_values)


def product_kernel(homes, rows, slots, index_ref, tiles_ref, scale_ref, *refs):
    units = refs[:-3]
    out_ref, source_ref, gathered_ref = refs[-3:]
    lane = lax.broadcasted_iota(jnp.int32, (HALF, 128), 1)
    left = lane < HALF
    for k, (which, first) in enumerate(homes):
        part = units[which][first:first + HALF]
        high = part.astype(jnp.bfloat16).astype(jnp.float32)
        low = part - high
        top = jnp.where(left, high, pltpu.roll(low, HALF, 1))
        bottom = jnp.where(left, pltpu.roll(high, HALF, 1), low)
        source_ref[k, 0:HALF] = top.astype(jnp.bfloat16)
        source_ref[k, HALF:128] = bottom.astype(jnp.bfloat16)
    source_ref[len(homes)] = jnp.zeros((128, 128), jnp.bfloat16)
    for i in range(rows):
        for s in range(slots):
            gathered_ref[i, s * 128:(s + 1) * 128] = source_ref[index_ref[i, s]]
    for i in range(rows):
        both = jnp.dot(tiles_ref[i], gathered_ref[i], preferred_element_type=jnp.float32)
        total = both[0:128] + both[128:256]
        total = total + pltpu.roll(total, HALF, 1)
        packed = jnp.where(left, total[0:HALF], total[HALF:128])
        out_ref[i * HALF:(i + 1) * HALF] = packed * scale_ref[i * HALF:(i + 1) * HALF]


def product(slot_index, tiles, scale, units, homes):
    rows, slots = slot_index.shape
    vmem = pl.BlockSpec(memory_space=pltpu.VMEM)
    return pl.pallas_call(
        functools.partial(product_kernel, homes, rows, slots),
        in_specs=[pl.BlockSpec(memory_space=pltpu.SMEM)] + [vmem] * (2 + len(units)),
        out_specs=vmem,
        out_shape=jax.ShapeDtypeStruct((rows * HALF, 128), jnp.float32),
        scratch_shapes=[
            pltpu.VMEM((len(homes) + 1, 128, 128), jnp.bfloat16),
            pltpu.VMEM((rows, slots * 128, 128), jnp.bfloat16),
        ],
        compiler_params=pltpu.CompilerParams(vmem_limit_bytes=32 * 2**20),
        cost_estimate=pl.CostEstimate(flops=2 * rows * slots * 256 * 128 * 128, bytes_accessed=8 * 2**20, transcendentals=0),
    )(slot_index, tiles, scale, *units)


def finish_kernel(ordered_ref, root_ref, *refs):
    out_ref = refs[-1]
    fields = refs[:-1]
    out_ref[0] = ordered_ref[...]
    lane = lax.broadcasted_iota(jnp.int32, (HALF, 128), 1)
    left = lane < HALF
    blocks = ordered_ref.shape[0] // 128
    for hop in range(HOPS):
        for b in range(blocks):
            a = fields[2 * hop][b * HALF:(b + 1) * HALF]
            c = fields[2 * hop + 1][b * HALF:(b + 1) * HALF]
            first = b * 128
            top = jnp.where(left, a, pltpu.roll(c, HALF, 1))
            bottom = jnp.where(left, pltpu.roll(a, HALF, 1), c)
            out_ref[hop + 1, first:first + HALF] = top * root_ref[first:first + HALF]
            out_ref[hop + 1, first + HALF:first + 128] = bottom * root_ref[first + HALF:first + 128]


def finish(ordered, root, fields):
    vmem = pl.BlockSpec(memory_space=pltpu.VMEM)
    return pl.pallas_call(
        finish_kernel,
        in_specs=[vmem] * (2 + len(fields)),
        out_specs=vmem,
        out_shape=jax.ShapeDtypeStruct((HOPS + 1,) + ordered.shape, jnp.float32),
        compiler_params=pltpu.CompilerParams(vmem_limit_bytes=32 * 2**20),
    )(ordered, root, *fields)


def window(own):
    two, six, four = ahead(own, 2), ahead(own, 6), ahead(own, 4)
    near = ahead(jnp.concatenate([own, six]), 1)
    far = ahead(jnp.concatenate([four, six]), -1)
    arrays = [own, two, four, six, near, far]
    places = [(0, 0), (4, 0), (1, 0), (5, 0), (2, 0), (5, 1), (3, 0), (4, 1)]
    return arrays, places


def local(features, tile_values, tile_cols, tile_counts, degrees, curve_order):
    rank_blk = lax.axis_index("blk")
    rank_rep = lax.axis_index("rep")
    cycle = lax.axis_size("blk")
    span = cycle // lax.axis_size("rep")
    rows, slots = tile_values.shape[:2]
    ordered = jnp.take(features, curve_order - rank_blk * features.shape[0], axis=0, mode="clip")
    count = degrees.astype(jnp.float32)
    inv_root = lax.rsqrt(count)[:, None]
    wide = jnp.broadcast_to(inv_root, features.shape)
    root = jnp.broadcast_to(count[:, None], features.shape) * wide
    scales = [pack(wide * wide, chain) for chain in range(CHAINS)]
    source = tile_cols // rows
    distance = jnp.clip(jnp.mod(rank_blk - rank_rep * span - source, cycle), 0, span - 1)
    live = jnp.arange(slots, dtype=jnp.int32)[None, :] < tile_counts
    slot_index = jnp.where(live, distance * rows + tile_cols % rows, span * rows)
    tiles = tile_parts(tile_values)

    def partials(owns):
        out = []
        for chain, own in enumerate(owns):
            arrays, places = window(own)
            size = rows * HALF
            homes = tuple((which, at * size + b * HALF) for which, at in places for b in range(rows))
            out.append(product(slot_index, tiles, scales[chain], arrays, homes))
        return out

    def core_pair(part):
        return part + send(part, lambda p, w: (p, w ^ 1))

    def near_chip(part):
        return part + send(part, lambda p, w: (p, w ^ 2))

    def align(pair_sum):
        same = send(pair_sum, lambda p, w: (p + span * w, w))

        def other(p, v):
            w = 6 - (v & 6) + (v & 1)
            return p + span * w, w

        return same + send(pair_sum, other)

    sent = wide * ordered
    owns = [send(pack(sent, chain), lambda p, w: (p + span * w, w)) for chain in range(CHAINS)]
    kept = []
    for hop in range(HOPS):
        parts = partials(owns)
        sums = [near_chip(core_pair(part)) for part in parts]
        if hop < HOPS - 1:
            owns = [align(s) for s in sums]
            kept += owns
    last = [s + send(s, lambda p, w: (p, w ^ 4)) for s in sums]
    size = rows * HALF
    back = send(jnp.concatenate(kept), lambda p, w: (p - span * w, w))
    fields = [back[n * size:(n + 1) * size] for n in range(len(kept))] + last
    return finish(ordered, root, fields)


def solution(mesh):
    return jax.shard_map(
        local,
        mesh=mesh,
        in_specs=(
            P("blk", None),
            P("blk", "rep", None, None),
            P("blk", "rep"),
            P("blk", "rep"),
            P("blk"),
            P("blk"),
        ),
        out_specs=P(None, "blk", None),
        check_vma=False,
    )
```

```python
import functools

import jax
import jax.numpy as jnp
from jax import lax
from jax.experimental import pallas as pl
from jax.experimental.pallas import tpu as pltpu
from jax.sharding import PartitionSpec as P

HOPS = 4
HALF = 64
VMEM_BYTES = 16 * 2**20


def send(block, place):
    cycle, groups = lax.axis_size("blk"), lax.axis_size("rep")
    route = []
    for p in range(cycle):
        for w in range(groups):
            to_p, to_w = place(p, w)
            route.append((p * groups + w, (to_p % cycle) * groups + to_w))
    return lax.ppermute(block, ("blk", "rep"), route)


def swap_cores(block):
    return send(block, lambda p, w: (p, w ^ 1))


def pack(field, half):
    blocks = field.shape[0] // 128
    part = field.reshape(blocks, 2, HALF, 2, HALF)[:, :, :, half]
    return part.transpose(0, 2, 1, 3).reshape(blocks * HALF, 128)


def split_tiles(first_slots, second_slots, core_ref, mine_ref, other_ref, out_ref):
    for s, (at_first, at_second) in enumerate(zip(first_slots, second_slots)):
        def read(at):
            held, place = at
            return (mine_ref if held == "mine" else other_ref)[place * 128:(place + 1) * 128]
        tile = jnp.where(core_ref[0] == 0, read(at_first), read(at_second))
        high = tile.astype(jnp.bfloat16)
        low = (tile - high.astype(jnp.float32)).astype(jnp.bfloat16)
        out_ref[0, 0:128, s * 128:(s + 1) * 128] = high
        out_ref[0, 128:256, s * 128:(s + 1) * 128] = low


def tile_parts(core, mine, other, rows, first_slots, second_slots):
    slots = len(first_slots)
    held = 1 + max(place for _, place in first_slots)
    block = pl.BlockSpec((held * 128, 128), lambda i, core: (i, 0))
    return pl.pallas_call(
        functools.partial(split_tiles, first_slots, second_slots),
        grid_spec=pltpu.PrefetchScalarGridSpec(
            num_scalar_prefetch=1,
            grid=(rows,),
            in_specs=[block, block],
            out_specs=pl.BlockSpec((1, 256, slots * 128), lambda i, core: (i, 0, 0)),
        ),
        out_shape=jax.ShapeDtypeStruct((rows, 256, slots * 128), jnp.bfloat16),
        compiler_params=pltpu.CompilerParams(vmem_limit_bytes=VMEM_BYTES),
    )(core, mine, other)


def multiply(index_ref, tiles_ref, scale_ref, source_ref, gathered_ref, out_ref):
    rows, slots = index_ref.shape
    left = lax.broadcasted_iota(jnp.int32, (HALF, 128), 1) < HALF
    for i in range(rows):
        for s in range(slots):
            gathered_ref[i, s * 128:(s + 1) * 128] = source_ref[index_ref[i, s]]
    for i in range(rows):
        both = jnp.dot(tiles_ref[i], gathered_ref[i], preferred_element_type=jnp.float32)
        total = both[0:128] + both[128:256]
        total = total + pltpu.roll(total, HALF, 1)
        at = slice(i * HALF, (i + 1) * HALF)
        out_ref[at] = jnp.where(left, total[0:HALF], total[HALF:128]) * scale_ref[at]


def near_kernel(index_ref, tiles_ref, scale_ref, units_ref, near_ref, source_ref, gathered_ref):
    left = lax.broadcasted_iota(jnp.int32, (HALF, 128), 1) < HALF
    count = units_ref.shape[0] // HALF
    for k in range(count):
        part = units_ref[k * HALF:(k + 1) * HALF]
        high = part.astype(jnp.bfloat16).astype(jnp.float32)
        low = part - high
        top = jnp.where(left, high, pltpu.roll(low, HALF, 1))
        bottom = jnp.where(left, pltpu.roll(high, HALF, 1), low)
        source_ref[k, 0:HALF] = top.astype(jnp.bfloat16)
        source_ref[k, HALF:128] = bottom.astype(jnp.bfloat16)
    source_ref[count] = jnp.zeros((128, 128), jnp.bfloat16)
    multiply(index_ref, tiles_ref, scale_ref, source_ref, gathered_ref, near_ref)


def far_kernel(members, index_ref, tiles_ref, scale_ref, source_ref, near_ref, out_ref, gathered_ref, far_ref):
    multiply(index_ref, tiles_ref, scale_ref, source_ref, gathered_ref, far_ref)
    piece = near_ref.shape[0] // members
    for m in range(members):
        at = slice(m * piece, (m + 1) * piece)
        out_ref[2 * m * piece:(2 * m + 1) * piece] = near_ref[at]
        out_ref[(2 * m + 1) * piece:(2 * m + 2) * piece] = far_ref[at]


def product_call(kernel, inputs, rows, slots, out_shape, more_scratch=()):
    vmem = pl.BlockSpec(memory_space=pltpu.VMEM)
    smem = pl.BlockSpec(memory_space=pltpu.SMEM)
    return pl.pallas_call(
        kernel,
        in_specs=[smem] + [vmem] * (inputs - 1),
        out_specs=jax.tree.map(lambda _: vmem, out_shape),
        out_shape=out_shape,
        scratch_shapes=[pltpu.VMEM((rows, slots * 128, 128), jnp.bfloat16), *more_scratch],
        compiler_params=pltpu.CompilerParams(vmem_limit_bytes=VMEM_BYTES),
        cost_estimate=pl.CostEstimate(flops=2 * rows * slots * 256 * 128 * 128, bytes_accessed=4 * 2**20, transcendentals=0),
    )


def near_product(index, tiles, scale, units):
    rows, slots = index.shape
    sums = jax.ShapeDtypeStruct((rows * HALF, 128), jnp.float32)
    source = jax.ShapeDtypeStruct((units.shape[0] // HALF + 1, 128, 128), jnp.bfloat16)
    return product_call(near_kernel, 4, rows, slots, [sums, source])(index, tiles, scale, units)


def far_product(index, tiles, scale, source, near, members):
    rows, slots = index.shape
    both = jax.ShapeDtypeStruct((2 * rows * HALF, 128), jnp.float32)
    scratch = [pltpu.VMEM((rows * HALF, 128), jnp.float32)]
    return product_call(functools.partial(far_kernel, members), 5, rows, slots, both, scratch)(index, tiles, scale, source, near)


def piece_sums(came_ref, lines, pairs):
    piece = came_ref.shape[0] // (2 * lines * pairs)

    def read(line, pair, which):
        first = (2 * (line * pairs + pair) + which) * piece
        return came_ref[first:first + piece]

    sums = []
    for line in range(lines):
        terms = [read(line, pair, 0) for pair in range(pairs)]
        terms += [read((line - 1) % lines, pair, 1) for pair in range(pairs)]
        while len(terms) > 1:
            terms = [a + b for a, b in zip(terms[::2], terms[1::2])]
        sums.append(terms[0])
    return sums


def hand_on_kernel(lines, pairs, came_ref, out_ref):
    sums = piece_sums(came_ref, lines, pairs)
    piece = sums[0].shape[0]
    for line in range(lines):
        for pair in range(pairs):
            first = 2 * (line * pairs + pair) * piece
            out_ref[first:first + piece] = sums[(line - 2 * pair) % lines]
            out_ref[first + piece:first + 2 * piece] = sums[(line - 2 * pair - 1) % lines]


def hand_out_kernel(lines, pairs, came_ref, out_ref):
    sums = piece_sums(came_ref, lines, pairs)
    piece = sums[0].shape[0]
    for line in range(lines):
        for member in range(2 * pairs):
            first = (line * 2 * pairs + member) * piece
            out_ref[first:first + piece] = sums[line]


def hand(kernel, came, lines, pairs):
    vmem = pl.BlockSpec(memory_space=pltpu.VMEM)
    return pl.pallas_call(
        functools.partial(kernel, lines, pairs),
        in_specs=[vmem],
        out_specs=vmem,
        out_shape=jax.ShapeDtypeStruct(came.shape, jnp.float32),
        compiler_params=pltpu.CompilerParams(vmem_limit_bytes=VMEM_BYTES),
    )(came)


def choose_kernel(members, span, rank_ref, came_ref, chunks_ref, own_ref, behind_ref):
    piece = came_ref.shape[0] // (2 * members)
    for m in range(members):
        at = slice(m * piece, (m + 1) * piece)
        own_ref[at] = came_ref[2 * m * piece:(2 * m + 1) * piece]
        behind_ref[at] = came_ref[(2 * m + 1) * piece:(2 * m + 2) * piece]
    for y in range(span):
        chunks_ref[y] = jnp.where(y >= rank_ref[0], own_ref[...], behind_ref[...])


def choose(rank_y, came, members, span):
    vmem = pl.BlockSpec(memory_space=pltpu.VMEM)
    unit = (came.shape[0] // 2, came.shape[1])
    return pl.pallas_call(
        functools.partial(choose_kernel, members, span),
        in_specs=[pl.BlockSpec(memory_space=pltpu.SMEM), vmem],
        out_specs=[vmem, vmem],
        out_shape=[jax.ShapeDtypeStruct((span, *unit), jnp.float32), jax.ShapeDtypeStruct(unit, jnp.float32)],
        scratch_shapes=[pltpu.VMEM(unit, jnp.float32)],
        compiler_params=pltpu.CompilerParams(vmem_limit_bytes=VMEM_BYTES),
    )(rank_y, came)


def finish_kernel(members, core_ref, ordered_ref, root_ref, mine_ref, other_ref, last_ref, out_ref, halves_ref):
    out_ref[0] = ordered_ref[...]
    left = lax.broadcasted_iota(jnp.int32, (HALF, 128), 1) < HALF
    first_core = core_ref[0] == 0
    blocks = ordered_ref.shape[0] // 128
    size = blocks * HALF
    piece = size // members
    for m in range(members):
        for half in range(2):
            first = (2 * m + half) * piece
            halves_ref[half, m * piece:(m + 1) * piece] = last_ref[first:first + piece]
    for hop in range(HOPS):
        for b in range(blocks):
            if hop < HOPS - 1:
                at = slice(hop * size + b * HALF, hop * size + (b + 1) * HALF)
                a = jnp.where(first_core, mine_ref[at], other_ref[at])
                c = jnp.where(first_core, other_ref[at], mine_ref[at])
            else:
                at = slice(b * HALF, (b + 1) * HALF)
                a, c = halves_ref[0, at], halves_ref[1, at]
            first = b * 128
            top = jnp.where(left, a, pltpu.roll(c, HALF, 1))
            bottom = jnp.where(left, pltpu.roll(a, HALF, 1), c)
            out_ref[hop + 1, first:first + HALF] = top * root_ref[first:first + HALF]
            out_ref[hop + 1, first + HALF:first + 128] = bottom * root_ref[first + HALF:first + 128]


def finish(core, ordered, root, mine, other, last, members):
    vmem = pl.BlockSpec(memory_space=pltpu.VMEM)
    return pl.pallas_call(
        functools.partial(finish_kernel, members),
        in_specs=[pl.BlockSpec(memory_space=pltpu.SMEM)] + [vmem] * 5,
        out_specs=vmem,
        out_shape=jax.ShapeDtypeStruct((HOPS + 1,) + ordered.shape, jnp.float32),
        scratch_shapes=[pltpu.VMEM((2, ordered.shape[0] // 2, 128), jnp.float32)],
        compiler_params=pltpu.CompilerParams(vmem_limit_bytes=VMEM_BYTES),
    )(core, ordered, root, mine, other, last)


def ring_exchange(chunks):
    span = chunks.shape[0]
    rings = [[first + at for at in range(span)] for first in range(0, lax.axis_size("blk"), span)]
    return lax.all_to_all(chunks, "blk", 0, 0, axis_index_groups=rings)


def plane_exchange(block, span, cores):
    cycle, groups = lax.axis_size("blk"), lax.axis_size("rep")
    planes = []
    for y in range(span):
        for core in range(0, 2, cores):
            starts = range(core, groups, 2) if cores == 1 else range(groups)
            planes.append([p * groups + w for p in range(y, cycle, span) for w in starts])
    pieces = block.reshape(len(planes[0]), 1, -1)
    moved = lax.all_to_all(pieces, ("blk", "rep"), 0, 0, axis_index_groups=planes)
    return moved.reshape(block.shape)


def local(features, tile_values, tile_cols, tile_counts, degrees, curve_order):
    rank_blk = lax.axis_index("blk")
    rank_rep = lax.axis_index("rep")
    span = lax.axis_size("blk") // lax.axis_size("rep")
    rows, slots = tile_values.shape[:2]
    mid = slots // 2
    core = rank_rep % 2
    first_core = core == 0
    core_ref = core.reshape(1)

    swapped = swap_cores(tile_values)
    live = jnp.arange(slots, dtype=jnp.int32)[None, :] < tile_counts
    index = jnp.where(live, tile_cols % (span * rows), span * rows)
    swapped_index = swap_cores(index)
    near_index = jnp.where(first_core, index, swapped_index)
    leaving = jnp.where(first_core, swapped[:, :mid], tile_values[:, mid:]).reshape(-1, 128)
    leaving_index = jnp.where(first_core, swapped_index, index).astype(jnp.float32)
    index_rows = jnp.pad(leaving_index, ((0, 8 - rows), (0, 128 - slots)))
    leaving = jnp.concatenate([leaving, index_rows])

    ordered = jnp.take(features, curve_order - rank_blk * features.shape[0], axis=0, mode="clip")
    count = degrees.astype(jnp.float32)
    inv_root = lax.rsqrt(count)[:, None]
    wide = jnp.broadcast_to(inv_root, features.shape)
    root = jnp.broadcast_to(count[:, None], features.shape) * wide
    scale = pack(wide * wide, 0)
    sent = wide * ordered
    start = jnp.where(first_core, pack(sent, 0), pack(sent, 1))

    def aligned(p, w):
        return p + 2 * span * (w // 2), w

    def behind_aligned(p, w):
        return p + 2 * span * (w // 2) + span, w

    rank_y = rank_blk % span
    lines = lax.axis_size("blk") // span
    pairs = lax.axis_size("rep") // 2
    members = lines * pairs
    own, behind = send(start, aligned), send(start, behind_aligned)
    far_scale = send(scale, lambda p, w: (p - span, w))
    every = [("mine", s) for s in range(slots)], [("other", s) for s in range(slots)]
    flat = tile_values.reshape(-1, 128), swapped.reshape(-1, 128)
    near_tiles = tile_parts(core_ref, *flat, rows, *every)
    own, behind, leaving, far_scale = lax.optimization_barrier((own, behind, leaving, far_scale))
    came = send(leaving, lambda p, w: (p - span, w))
    ring = jnp.arange(span, dtype=jnp.int32)[:, None, None]
    chunks = jnp.where(ring >= rank_y, own[None], behind[None])
    kept = []
    for hop in range(HOPS):
        units = ring_exchange(chunks).reshape(-1, 128)
        if hop == 0:
            units, came = lax.optimization_barrier((units, came))
        near, source = near_product(near_index, near_tiles, scale, units)
        if hop == 0:
            rest = swap_cores(came)
            low_slots = [("mine", s) for s in range(mid)] + [("other", s) for s in range(mid)]
            high_slots = [("other", s) for s in range(mid)] + [("mine", s) for s in range(mid)]
            far_index = came[rows * mid * 128:][:rows, :slots].astype(jnp.int32)
            far_tiles = tile_parts(core_ref, came, rest, rows, low_slots, high_slots)
        sums = far_product(far_index, far_tiles, far_scale, source, near, members)
        pieces = plane_exchange(sums, span, 1)
        if hop < HOPS - 1:
            came_units = plane_exchange(hand(hand_on_kernel, pieces, lines, pairs), span, 1)
            chunks, own = choose(rank_y.reshape(1), came_units, members, span)
            kept.append(own)
    last = plane_exchange(hand(hand_out_kernel, pieces, lines, pairs), span, 2)
    mine = send(jnp.concatenate(kept), lambda p, w: (p - 2 * span * (w // 2), w))
    return finish(core_ref, ordered, root, mine, swap_cores(mine), last, members)


def solution(mesh):
    return jax.shard_map(
        local,
        mesh=mesh,
        in_specs=(
            P("blk", None),
            P("blk", "rep", None, None),
            P("blk", "rep"),
            P("blk", "rep"),
            P("blk"),
            P("blk"),
        ),
        out_specs=P(None, "blk", None),
        check_vma=False,
    )
```

```python
import functools

import jax
import jax.numpy as jnp
from jax import lax
from jax.experimental import pallas as pl
from jax.experimental.pallas import tpu as pltpu
from jax.sharding import PartitionSpec as P

HOPS = 4
HALF = 64
VMEM_BYTES = 16 * 2**20


def send(block, place):
    cycle, groups = lax.axis_size("blk"), lax.axis_size("rep")
    route = []
    for p in range(cycle):
        for w in range(groups):
            to_p, to_w = place(p, w)
            route.append((p * groups + w, (to_p % cycle) * groups + to_w))
    return lax.ppermute(block, ("blk", "rep"), route)


def swap_cores(block):
    return send(block, lambda p, w: (p, w ^ 1))


def pack(field, half):
    blocks = field.shape[0] // 128
    part = field.reshape(blocks, 2, HALF, 2, HALF)[:, :, :, half]
    return part.transpose(0, 2, 1, 3).reshape(blocks * HALF, 128)


def split_tiles(first_slots, second_slots, core_ref, mine_ref, other_ref, out_ref):
    for s, (at_first, at_second) in enumerate(zip(first_slots, second_slots)):
        def read(at):
            held, place = at
            return (mine_ref if held == "mine" else other_ref)[place * 128:(place + 1) * 128]
        tile = jnp.where(core_ref[0] == 0, read(at_first), read(at_second))
        high = tile.astype(jnp.bfloat16)
        low = (tile - high.astype(jnp.float32)).astype(jnp.bfloat16)
        out_ref[0, 0:128, s * 128:(s + 1) * 128] = high
        out_ref[0, 128:256, s * 128:(s + 1) * 128] = low


def tile_parts(core, mine, other, rows, first_slots, second_slots):
    slots = len(first_slots)
    held = 1 + max(place for _, place in first_slots)
    block = pl.BlockSpec((held * 128, 128), lambda i, core: (i, 0))
    return pl.pallas_call(
        functools.partial(split_tiles, first_slots, second_slots),
        grid_spec=pltpu.PrefetchScalarGridSpec(
            num_scalar_prefetch=1,
            grid=(rows,),
            in_specs=[block, block],
            out_specs=pl.BlockSpec((1, 256, slots * 128), lambda i, core: (i, 0, 0)),
        ),
        out_shape=jax.ShapeDtypeStruct((rows, 256, slots * 128), jnp.bfloat16),
        compiler_params=pltpu.CompilerParams(vmem_limit_bytes=VMEM_BYTES),
    )(core, mine, other)


def multiply(index_ref, tiles_ref, scale_ref, source_ref, gathered_ref, out_ref):
    rows, slots = index_ref.shape
    left = lax.broadcasted_iota(jnp.int32, (HALF, 128), 1) < HALF
    for i in range(rows):
        for s in range(slots):
            gathered_ref[i, s * 128:(s + 1) * 128] = source_ref[index_ref[i, s]]
    for i in range(rows):
        both = jnp.dot(tiles_ref[i], gathered_ref[i], preferred_element_type=jnp.float32)
        total = both[0:128] + both[128:256]
        total = total + pltpu.roll(total, HALF, 1)
        at = slice(i * HALF, (i + 1) * HALF)
        out_ref[at] = jnp.where(left, total[0:HALF], total[HALF:128]) * scale_ref[at]


def near_kernel(index_ref, tiles_ref, scale_ref, units_ref, near_ref, source_ref, gathered_ref):
    left = lax.broadcasted_iota(jnp.int32, (HALF, 128), 1) < HALF
    count = units_ref.shape[0] // HALF
    for k in range(count):
        part = units_ref[k * HALF:(k + 1) * HALF]
        high = part.astype(jnp.bfloat16).astype(jnp.float32)
        low = part - high
        top = jnp.where(left, high, pltpu.roll(low, HALF, 1))
        bottom = jnp.where(left, pltpu.roll(high, HALF, 1), low)
        source_ref[k, 0:HALF] = top.astype(jnp.bfloat16)
        source_ref[k, HALF:128] = bottom.astype(jnp.bfloat16)
    source_ref[count] = jnp.zeros((128, 128), jnp.bfloat16)
    multiply(index_ref, tiles_ref, scale_ref, source_ref, gathered_ref, near_ref)


def last_kernel(index_ref, tiles_ref, scale_ref, source_ref, out_ref, gathered_ref):
    multiply(index_ref, tiles_ref, scale_ref, source_ref, gathered_ref, out_ref)


def far_kernel(members, index_ref, tiles_ref, scale_ref, source_ref, near_ref, out_ref, gathered_ref, far_ref):
    multiply(index_ref, tiles_ref, scale_ref, source_ref, gathered_ref, far_ref)
    piece = near_ref.shape[0] // members
    for m in range(members):
        at = slice(m * piece, (m + 1) * piece)
        out_ref[2 * m * piece:(2 * m + 1) * piece] = near_ref[at]
        out_ref[(2 * m + 1) * piece:(2 * m + 2) * piece] = far_ref[at]


def product_call(kernel, inputs, rows, slots, out_shape, more_scratch=()):
    vmem = pl.BlockSpec(memory_space=pltpu.VMEM)
    smem = pl.BlockSpec(memory_space=pltpu.SMEM)
    return pl.pallas_call(
        kernel,
        in_specs=[smem] + [vmem] * (inputs - 1),
        out_specs=jax.tree.map(lambda _: vmem, out_shape),
        out_shape=out_shape,
        scratch_shapes=[pltpu.VMEM((rows, slots * 128, 128), jnp.bfloat16), *more_scratch],
        compiler_params=pltpu.CompilerParams(vmem_limit_bytes=VMEM_BYTES),
        cost_estimate=pl.CostEstimate(flops=2 * rows * slots * 256 * 128 * 128, bytes_accessed=4 * 2**20, transcendentals=0),
    )


def near_product(index, tiles, scale, units):
    rows, slots = index.shape
    sums = jax.ShapeDtypeStruct((rows * HALF, 128), jnp.float32)
    source = jax.ShapeDtypeStruct((units.shape[0] // HALF + 1, 128, 128), jnp.bfloat16)
    return product_call(near_kernel, 4, rows, slots, [sums, source])(index, tiles, scale, units)


def far_product(index, tiles, scale, source, near, members):
    rows, slots = index.shape
    both = jax.ShapeDtypeStruct((2 * rows * HALF, 128), jnp.float32)
    scratch = [pltpu.VMEM((rows * HALF, 128), jnp.float32)]
    return product_call(functools.partial(far_kernel, members), 5, rows, slots, both, scratch)(index, tiles, scale, source, near)


def last_product(index, tiles, scale, source):
    rows, slots = index.shape
    sums = jax.ShapeDtypeStruct((rows * HALF, 128), jnp.float32)
    return product_call(last_kernel, 4, rows, slots, sums)(index, tiles, scale, source)


def piece_sums(came_ref, lines, pairs):
    piece = came_ref.shape[0] // (2 * lines * pairs)

    def read(line, pair, which):
        first = (2 * (line * pairs + pair) + which) * piece
        return came_ref[first:first + piece]

    sums = []
    for line in range(lines):
        terms = [read(line, pair, 0) for pair in range(pairs)]
        terms += [read((line - 1) % lines, pair, 1) for pair in range(pairs)]
        while len(terms) > 1:
            terms = [a + b for a, b in zip(terms[::2], terms[1::2])]
        sums.append(terms[0])
    return sums


def hand_on_kernel(lines, pairs, came_ref, out_ref):
    sums = piece_sums(came_ref, lines, pairs)
    piece = sums[0].shape[0]
    for line in range(lines):
        for pair in range(pairs):
            first = 2 * (line * pairs + pair) * piece
            out_ref[first:first + piece] = sums[(line - 2 * pair) % lines]
            out_ref[first + piece:first + 2 * piece] = sums[(line - 2 * pair - 1) % lines]


def hand_on(came, lines, pairs):
    vmem = pl.BlockSpec(memory_space=pltpu.VMEM)
    return pl.pallas_call(
        functools.partial(hand_on_kernel, lines, pairs),
        in_specs=[vmem],
        out_specs=vmem,
        out_shape=jax.ShapeDtypeStruct(came.shape, jnp.float32),
        compiler_params=pltpu.CompilerParams(vmem_limit_bytes=VMEM_BYTES),
    )(came)


def choose_kernel(members, span, rank_ref, came_ref, chunks_ref, own_ref, behind_ref):
    piece = came_ref.shape[0] // (2 * members)
    for m in range(members):
        at = slice(m * piece, (m + 1) * piece)
        own_ref[at] = came_ref[2 * m * piece:(2 * m + 1) * piece]
        behind_ref[at] = came_ref[(2 * m + 1) * piece:(2 * m + 2) * piece]
    for y in range(span):
        chunks_ref[y] = jnp.where(y >= rank_ref[0], own_ref[...], behind_ref[...])


def choose(rank_y, came, members, span):
    vmem = pl.BlockSpec(memory_space=pltpu.VMEM)
    unit = (came.shape[0] // 2, came.shape[1])
    return pl.pallas_call(
        functools.partial(choose_kernel, members, span),
        in_specs=[pl.BlockSpec(memory_space=pltpu.SMEM), vmem],
        out_specs=[vmem, vmem],
        out_shape=[jax.ShapeDtypeStruct((span, *unit), jnp.float32), jax.ShapeDtypeStruct(unit, jnp.float32)],
        scratch_shapes=[pltpu.VMEM(unit, jnp.float32)],
        compiler_params=pltpu.CompilerParams(vmem_limit_bytes=VMEM_BYTES),
    )(rank_y, came)


def finish_kernel(core_ref, ordered_ref, root_ref, mine_ref, mine_last_ref, other_ref, other_last_ref, out_ref):
    out_ref[0] = ordered_ref[...]
    left = lax.broadcasted_iota(jnp.int32, (HALF, 128), 1) < HALF
    first_core = core_ref[0] == 0
    blocks = ordered_ref.shape[0] // 128
    size = blocks * HALF
    for hop in range(HOPS):
        for b in range(blocks):
            at = b * HALF if hop == HOPS - 1 else hop * size + b * HALF
            mine = (mine_last_ref if hop == HOPS - 1 else mine_ref)[at:at + HALF]
            other = (other_last_ref if hop == HOPS - 1 else other_ref)[at:at + HALF]
            a = jnp.where(first_core, mine, other)
            c = jnp.where(first_core, other, mine)
            first = b * 128
            top = jnp.where(left, a, pltpu.roll(c, HALF, 1))
            bottom = jnp.where(left, pltpu.roll(a, HALF, 1), c)
            out_ref[hop + 1, first:first + HALF] = top * root_ref[first:first + HALF]
            out_ref[hop + 1, first + HALF:first + 128] = bottom * root_ref[first + HALF:first + 128]


def finish(core, ordered, root, fields):
    vmem = pl.BlockSpec(memory_space=pltpu.VMEM)
    return pl.pallas_call(
        finish_kernel,
        in_specs=[pl.BlockSpec(memory_space=pltpu.SMEM)] + [vmem] * (2 + len(fields)),
        out_specs=vmem,
        out_shape=jax.ShapeDtypeStruct((HOPS + 1,) + ordered.shape, jnp.float32),
        compiler_params=pltpu.CompilerParams(vmem_limit_bytes=VMEM_BYTES),
    )(core, ordered, root, *fields)


def ring_exchange(chunks):
    span = chunks.shape[0]
    rings = [[first + at for at in range(span)] for first in range(0, lax.axis_size("blk"), span)]
    return lax.all_to_all(chunks, "blk", 0, 0, axis_index_groups=rings)


def pair_exchange(block, pairs):
    cycle, groups = lax.axis_size("blk"), lax.axis_size("rep")
    sets = [[p * groups + w for w in range(core, groups, 2)] for p in range(cycle) for core in range(2)]
    copies = jnp.broadcast_to(block[None], (pairs, *block.shape))
    return lax.all_to_all(copies, ("blk", "rep"), 0, 0, axis_index_groups=sets)


def plane_exchange(block, span):
    cycle, groups = lax.axis_size("blk"), lax.axis_size("rep")
    planes = [
        [p * groups + w for p in range(y, cycle, span) for w in range(core, groups, 2)]
        for y in range(span) for core in range(2)
    ]
    pieces = block.reshape(len(planes[0]), 1, -1)
    moved = lax.all_to_all(pieces, ("blk", "rep"), 0, 0, axis_index_groups=planes)
    return moved.reshape(block.shape)


def local(features, tile_values, tile_cols, tile_counts, degrees, curve_order):
    rank_blk = lax.axis_index("blk")
    rank_rep = lax.axis_index("rep")
    span = lax.axis_size("blk") // lax.axis_size("rep")
    rows, slots = tile_values.shape[:2]
    mid = slots // 2
    core = rank_rep % 2
    first_core = core == 0
    core_ref = core.reshape(1)

    swapped = swap_cores(tile_values)
    live = jnp.arange(slots, dtype=jnp.int32)[None, :] < tile_counts
    index = jnp.where(live, tile_cols % (span * rows), span * rows)
    swapped_index = swap_cores(index)
    near_index = jnp.where(first_core, index, swapped_index)
    leaving = jnp.where(first_core, swapped[:, :mid], tile_values[:, mid:]).reshape(-1, 128)

    ordered = jnp.take(features, curve_order - rank_blk * features.shape[0], axis=0, mode="clip")
    count = degrees.astype(jnp.float32)
    inv_root = lax.rsqrt(count)[:, None]
    wide = jnp.broadcast_to(inv_root, features.shape)
    root = jnp.broadcast_to(count[:, None], features.shape) * wide
    scale = pack(wide * wide, 0)
    sent = wide * ordered
    start = jnp.where(first_core, pack(sent, 0), pack(sent, 1))

    def aligned(p, w):
        return p + 2 * span * (w // 2), w

    def behind_aligned(p, w):
        return p + 2 * span * (w // 2) + span, w

    rank_y = rank_blk % span
    lines = lax.axis_size("blk") // span
    pairs = lax.axis_size("rep") // 2
    members = lines * pairs
    own, behind = send(start, aligned), send(start, behind_aligned)
    leaving_index = jnp.where(first_core, swapped_index, index).astype(jnp.float32)
    index_rows = jnp.pad(leaving_index, ((0, 8 - rows), (0, 128 - slots)))
    far_parts = send(jnp.concatenate([scale, index_rows]), lambda p, w: (p - span, w))
    own, behind, far_parts, leaving = lax.optimization_barrier((own, behind, far_parts, leaving))
    came = send(leaving, lambda p, w: (p - span, w))
    far_scale = far_parts[:rows * HALF]
    far_index = far_parts[rows * HALF:][:rows, :slots].astype(jnp.int32)
    every = [("mine", s) for s in range(slots)], [("other", s) for s in range(slots)]
    flat = tile_values.reshape(-1, 128), swapped.reshape(-1, 128)
    near_tiles = tile_parts(core_ref, *flat, rows, *every)
    ring = jnp.arange(span, dtype=jnp.int32)[:, None, None]
    chunks = jnp.where(ring >= rank_y, own[None], behind[None])
    kept = []
    for hop in range(HOPS - 1):
        units = ring_exchange(chunks).reshape(-1, 128)
        if hop == 0:
            came, near_tiles = lax.optimization_barrier((came, near_tiles))
        near, source = near_product(near_index, near_tiles, scale, units)
        if hop == 0:
            rest = swap_cores(came)
            low_slots = [("mine", s) for s in range(mid)] + [("other", s) for s in range(mid)]
            high_slots = [("other", s) for s in range(mid)] + [("mine", s) for s in range(mid)]
            far_tiles = tile_parts(core_ref, came, rest, rows, low_slots, high_slots)
        sums = far_product(far_index, far_tiles, far_scale, source, near, members)
        pieces = plane_exchange(sums, span)
        came_units = plane_exchange(hand_on(pieces, lines, pairs), span)
        chunks, own = choose(rank_y.reshape(1), came_units, members, span)
        kept.append(own)
    mine = send(jnp.concatenate(kept), lambda p, w: (p - 2 * span * (w // 2), w))
    units = ring_exchange(chunks).reshape(-1, 128)
    near, source = near_product(near_index, near_tiles, scale, units)
    far = last_product(far_index, far_tiles, far_scale, source)
    chip = near + send(far, lambda p, w: (p + span, w))
    last = pair_exchange(chip, pairs).sum(axis=0)
    return finish(core_ref, ordered, root, [mine, last, swap_cores(mine), swap_cores(last)])


def solution(mesh):
    return jax.shard_map(
        local,
        mesh=mesh,
        in_specs=(
            P("blk", None),
            P("blk", "rep", None, None),
            P("blk", "rep"),
            P("blk", "rep"),
            P("blk"),
            P("blk"),
        ),
        out_specs=P(None, "blk", None),
        check_vma=False,
    )
```

```python
import functools

import jax
import jax.numpy as jnp
from jax import lax
from jax.experimental import pallas as pl
from jax.experimental.pallas import tpu as pltpu
from jax.sharding import PartitionSpec as P

HOPS = 4
HALF = 64
VMEM_BYTES = 16 * 2**20


def send(block, place):
    cycle, groups = lax.axis_size("blk"), lax.axis_size("rep")
    route = []
    for p in range(cycle):
        for w in range(groups):
            to_p, to_w = place(p, w)
            route.append((p * groups + w, (to_p % cycle) * groups + to_w))
    return lax.ppermute(block, ("blk", "rep"), route)


def swap_cores(block):
    return send(block, lambda p, w: (p, w ^ 1))


def pack(field, half):
    blocks = field.shape[0] // 128
    part = field.reshape(blocks, 2, HALF, 2, HALF)[:, :, :, half]
    return part.transpose(0, 2, 1, 3).reshape(blocks * HALF, 128)


def split_tiles(first_slots, second_slots, core_ref, mine_ref, other_ref, out_ref):
    for s, (at_first, at_second) in enumerate(zip(first_slots, second_slots)):
        def read(at):
            held, place = at
            return (mine_ref if held == "mine" else other_ref)[place * 128:(place + 1) * 128]
        tile = jnp.where(core_ref[0] == 0, read(at_first), read(at_second))
        high = tile.astype(jnp.bfloat16)
        low = (tile - high.astype(jnp.float32)).astype(jnp.bfloat16)
        out_ref[0, 0:128, s * 128:(s + 1) * 128] = high
        out_ref[0, 128:256, s * 128:(s + 1) * 128] = low


def tile_parts(core, mine, other, rows, first_slots, second_slots):
    slots = len(first_slots)
    held = 1 + max(place for _, place in first_slots)
    block = pl.BlockSpec((held * 128, 128), lambda i, core: (i, 0))
    return pl.pallas_call(
        functools.partial(split_tiles, first_slots, second_slots),
        grid_spec=pltpu.PrefetchScalarGridSpec(
            num_scalar_prefetch=1,
            grid=(rows,),
            in_specs=[block, block],
            out_specs=pl.BlockSpec((1, 256, slots * 128), lambda i, core: (i, 0, 0)),
        ),
        out_shape=jax.ShapeDtypeStruct((rows, 256, slots * 128), jnp.bfloat16),
        compiler_params=pltpu.CompilerParams(vmem_limit_bytes=VMEM_BYTES),
    )(core, mine, other)


def multiply(index_ref, tiles_ref, scale_ref, source_ref, gathered_ref, out_ref):
    rows, slots = index_ref.shape
    left = lax.broadcasted_iota(jnp.int32, (HALF, 128), 1) < HALF
    for i in range(rows):
        for s in range(slots):
            gathered_ref[i, s * 128:(s + 1) * 128] = source_ref[index_ref[i, s]]
    for i in range(rows):
        both = jnp.dot(tiles_ref[i], gathered_ref[i], preferred_element_type=jnp.float32)
        total = both[0:128] + both[128:256]
        total = total + pltpu.roll(total, HALF, 1)
        at = slice(i * HALF, (i + 1) * HALF)
        out_ref[at] = jnp.where(left, total[0:HALF], total[HALF:128]) * scale_ref[at]


def near_kernel(index_ref, tiles_ref, scale_ref, units_ref, near_ref, source_ref, gathered_ref):
    left = lax.broadcasted_iota(jnp.int32, (HALF, 128), 1) < HALF
    count = units_ref.shape[0] // HALF
    for k in range(count):
        part = units_ref[k * HALF:(k + 1) * HALF]
        high = part.astype(jnp.bfloat16).astype(jnp.float32)
        low = part - high
        top = jnp.where(left, high, pltpu.roll(low, HALF, 1))
        bottom = jnp.where(left, pltpu.roll(high, HALF, 1), low)
        source_ref[k, 0:HALF] = top.astype(jnp.bfloat16)
        source_ref[k, HALF:128] = bottom.astype(jnp.bfloat16)
    source_ref[count] = jnp.zeros((128, 128), jnp.bfloat16)
    multiply(index_ref, tiles_ref, scale_ref, source_ref, gathered_ref, near_ref)


def last_kernel(index_ref, tiles_ref, scale_ref, source_ref, out_ref, gathered_ref):
    multiply(index_ref, tiles_ref, scale_ref, source_ref, gathered_ref, out_ref)


def far_kernel(members, index_ref, tiles_ref, scale_ref, source_ref, near_ref, out_ref, gathered_ref, far_ref):
    multiply(index_ref, tiles_ref, scale_ref, source_ref, gathered_ref, far_ref)
    piece = near_ref.shape[0] // members
    for m in range(members):
        at = slice(m * piece, (m + 1) * piece)
        out_ref[2 * m * piece:(2 * m + 1) * piece] = near_ref[at]
        out_ref[(2 * m + 1) * piece:(2 * m + 2) * piece] = far_ref[at]


def product_call(kernel, inputs, rows, slots, out_shape, more_scratch=()):
    vmem = pl.BlockSpec(memory_space=pltpu.VMEM)
    smem = pl.BlockSpec(memory_space=pltpu.SMEM)
    return pl.pallas_call(
        kernel,
        in_specs=[smem] + [vmem] * (inputs - 1),
        out_specs=jax.tree.map(lambda _: vmem, out_shape),
        out_shape=out_shape,
        scratch_shapes=[pltpu.VMEM((rows, slots * 128, 128), jnp.bfloat16), *more_scratch],
        compiler_params=pltpu.CompilerParams(vmem_limit_bytes=VMEM_BYTES),
        cost_estimate=pl.CostEstimate(flops=2 * rows * slots * 256 * 128 * 128, bytes_accessed=4 * 2**20, transcendentals=0),
    )


def near_product(index, tiles, scale, units):
    rows, slots = index.shape
    sums = jax.ShapeDtypeStruct((rows * HALF, 128), jnp.float32)
    source = jax.ShapeDtypeStruct((units.shape[0] // HALF + 1, 128, 128), jnp.bfloat16)
    return product_call(near_kernel, 4, rows, slots, [sums, source])(index, tiles, scale, units)


def far_product(index, tiles, scale, source, near, members):
    rows, slots = index.shape
    both = jax.ShapeDtypeStruct((2 * rows * HALF, 128), jnp.float32)
    scratch = [pltpu.VMEM((rows * HALF, 128), jnp.float32)]
    return product_call(functools.partial(far_kernel, members), 5, rows, slots, both, scratch)(index, tiles, scale, source, near)


def last_product(index, tiles, scale, source):
    rows, slots = index.shape
    sums = jax.ShapeDtypeStruct((rows * HALF, 128), jnp.float32)
    return product_call(last_kernel, 4, rows, slots, sums)(index, tiles, scale, source)


def piece_sums(came_ref, lines, pairs):
    piece = came_ref.shape[0] // (2 * lines * pairs)

    def read(line, pair, which):
        first = (2 * (line * pairs + pair) + which) * piece
        return came_ref[first:first + piece]

    sums = []
    for line in range(lines):
        terms = [read(line, pair, 0) for pair in range(pairs)]
        terms += [read((line - 1) % lines, pair, 1) for pair in range(pairs)]
        while len(terms) > 1:
            terms = [a + b for a, b in zip(terms[::2], terms[1::2])]
        sums.append(terms[0])
    return sums


def hand_on_kernel(lines, pairs, came_ref, out_ref):
    sums = piece_sums(came_ref, lines, pairs)
    piece = sums[0].shape[0]
    for line in range(lines):
        for pair in range(pairs):
            first = 2 * (line * pairs + pair) * piece
            out_ref[first:first + piece] = sums[(line - 2 * pair) % lines]
            out_ref[first + piece:first + 2 * piece] = sums[(line - 2 * pair - 1) % lines]


def hand_on(came, lines, pairs):
    vmem = pl.BlockSpec(memory_space=pltpu.VMEM)
    return pl.pallas_call(
        functools.partial(hand_on_kernel, lines, pairs),
        in_specs=[vmem],
        out_specs=vmem,
        out_shape=jax.ShapeDtypeStruct(came.shape, jnp.float32),
        compiler_params=pltpu.CompilerParams(vmem_limit_bytes=VMEM_BYTES),
    )(came)


def choose_kernel(members, span, rank_ref, came_ref, chunks_ref, own_ref, behind_ref):
    piece = came_ref.shape[0] // (2 * members)
    for m in range(members):
        at = slice(m * piece, (m + 1) * piece)
        own_ref[at] = came_ref[2 * m * piece:(2 * m + 1) * piece]
        behind_ref[at] = came_ref[(2 * m + 1) * piece:(2 * m + 2) * piece]
    for y in range(span):
        chunks_ref[y] = jnp.where(y >= rank_ref[0], own_ref[...], behind_ref[...])


def choose(rank_y, came, members, span):
    vmem = pl.BlockSpec(memory_space=pltpu.VMEM)
    unit = (came.shape[0] // 2, came.shape[1])
    return pl.pallas_call(
        functools.partial(choose_kernel, members, span),
        in_specs=[pl.BlockSpec(memory_space=pltpu.SMEM), vmem],
        out_specs=[vmem, vmem],
        out_shape=[jax.ShapeDtypeStruct((span, *unit), jnp.float32), jax.ShapeDtypeStruct(unit, jnp.float32)],
        scratch_shapes=[pltpu.VMEM(unit, jnp.float32)],
        compiler_params=pltpu.CompilerParams(vmem_limit_bytes=VMEM_BYTES),
    )(rank_y, came)


def finish_kernel(core_ref, ordered_ref, root_ref, mine_ref, mine_last_ref, other_ref, other_last_ref, out_ref):
    out_ref[0] = ordered_ref[...]
    left = lax.broadcasted_iota(jnp.int32, (HALF, 128), 1) < HALF
    first_core = core_ref[0] == 0
    blocks = ordered_ref.shape[0] // 128
    size = blocks * HALF
    for hop in range(HOPS):
        for b in range(blocks):
            at = b * HALF if hop == HOPS - 1 else hop * size + b * HALF
            mine = (mine_last_ref if hop == HOPS - 1 else mine_ref)[at:at + HALF]
            other = (other_last_ref if hop == HOPS - 1 else other_ref)[at:at + HALF]
            a = jnp.where(first_core, mine, other)
            c = jnp.where(first_core, other, mine)
            first = b * 128
            top = jnp.where(left, a, pltpu.roll(c, HALF, 1))
            bottom = jnp.where(left, pltpu.roll(a, HALF, 1), c)
            out_ref[hop + 1, first:first + HALF] = top * root_ref[first:first + HALF]
            out_ref[hop + 1, first + HALF:first + 128] = bottom * root_ref[first + HALF:first + 128]


def finish(core, ordered, root, fields):
    vmem = pl.BlockSpec(memory_space=pltpu.VMEM)
    return pl.pallas_call(
        finish_kernel,
        in_specs=[pl.BlockSpec(memory_space=pltpu.SMEM)] + [vmem] * (2 + len(fields)),
        out_specs=vmem,
        out_shape=jax.ShapeDtypeStruct((HOPS + 1,) + ordered.shape, jnp.float32),
        compiler_params=pltpu.CompilerParams(vmem_limit_bytes=VMEM_BYTES),
    )(core, ordered, root, *fields)


def ring_exchange(chunks):
    span = chunks.shape[0]
    rings = [[first + at for at in range(span)] for first in range(0, lax.axis_size("blk"), span)]
    return lax.all_to_all(chunks, "blk", 0, 0, axis_index_groups=rings)


def pair_exchange(block, pairs):
    cycle, groups = lax.axis_size("blk"), lax.axis_size("rep")
    sets = [[p * groups + w for w in range(core, groups, 2)] for p in range(cycle) for core in range(2)]
    copies = jnp.broadcast_to(block[None], (pairs, *block.shape))
    return lax.all_to_all(copies, ("blk", "rep"), 0, 0, axis_index_groups=sets)


def plane_exchange(block, span):
    cycle, groups = lax.axis_size("blk"), lax.axis_size("rep")
    planes = [
        [p * groups + w for p in range(y, cycle, span) for w in range(core, groups, 2)]
        for y in range(span) for core in range(2)
    ]
    pieces = block.reshape(len(planes[0]), 1, -1)
    moved = lax.all_to_all(pieces, ("blk", "rep"), 0, 0, axis_index_groups=planes)
    return moved.reshape(block.shape)


def local(features, tile_values, tile_cols, tile_counts, degrees, curve_order):
    rank_blk = lax.axis_index("blk")
    rank_rep = lax.axis_index("rep")
    span = lax.axis_size("blk") // lax.axis_size("rep")
    rows, slots = tile_values.shape[:2]
    mid = slots // 2
    core = rank_rep % 2
    first_core = core == 0
    core_ref = core.reshape(1)

    swapped = swap_cores(tile_values)
    live = jnp.arange(slots, dtype=jnp.int32)[None, :] < tile_counts
    index = jnp.where(live, tile_cols % (span * rows), span * rows)
    swapped_index = swap_cores(index)
    near_index = jnp.where(first_core, index, swapped_index)
    leaving = jnp.where(first_core, swapped[:, :mid], tile_values[:, mid:]).reshape(-1, 128)

    ordered = jnp.take(features, curve_order - rank_blk * features.shape[0], axis=0, mode="clip")
    count = degrees.astype(jnp.float32)
    inv_root = lax.rsqrt(count)[:, None]
    wide = jnp.broadcast_to(inv_root, features.shape)
    root = jnp.broadcast_to(count[:, None], features.shape) * wide
    scale = pack(wide * wide, 0)
    sent = wide * ordered
    start = jnp.where(first_core, pack(sent, 0), pack(sent, 1))

    def aligned(p, w):
        return p + 2 * span * (w // 2), w

    def behind_aligned(p, w):
        return p + 2 * span * (w // 2) + span, w

    rank_y = rank_blk % span
    lines = lax.axis_size("blk") // span
    pairs = lax.axis_size("rep") // 2
    members = lines * pairs
    own, behind = send(start, aligned), send(start, behind_aligned)
    leaving_index = jnp.where(first_core, swapped_index, index).astype(jnp.float32)
    index_rows = jnp.pad(leaving_index, ((0, 8 - rows), (0, 128 - slots)))
    far_rows = jnp.concatenate([scale, index_rows])
    own, behind, leaving = lax.optimization_barrier((own, behind, leaving))
    came = send(leaving, lambda p, w: (p - span, w))
    every = [("mine", s) for s in range(slots)], [("other", s) for s in range(slots)]
    flat = tile_values.reshape(-1, 128), swapped.reshape(-1, 128)
    near_tiles = tile_parts(core_ref, *flat, rows, *every)
    near_tiles, far_rows = lax.optimization_barrier((near_tiles, far_rows))
    far_parts = send(far_rows, lambda p, w: (p - span, w))
    ring = jnp.arange(span, dtype=jnp.int32)[:, None, None]
    chunks = jnp.where(ring >= rank_y, own[None], behind[None])
    kept = []
    for hop in range(HOPS - 1):
        units = ring_exchange(chunks).reshape(-1, 128)
        if hop == 0:
            came, near_tiles, far_parts = lax.optimization_barrier((came, near_tiles, far_parts))
            far_scale = far_parts[:rows * HALF]
            far_index = far_parts[rows * HALF:][:rows, :slots].astype(jnp.int32)
        near, source = near_product(near_index, near_tiles, scale, units)
        if hop == 0:
            rest = swap_cores(came)
            low_slots = [("mine", s) for s in range(mid)] + [("other", s) for s in range(mid)]
            high_slots = [("other", s) for s in range(mid)] + [("mine", s) for s in range(mid)]
            far_tiles = tile_parts(core_ref, came, rest, rows, low_slots, high_slots)
        sums = far_product(far_index, far_tiles, far_scale, source, near, members)
        pieces = plane_exchange(sums, span)
        came_units = plane_exchange(hand_on(pieces, lines, pairs), span)
        chunks, own = choose(rank_y.reshape(1), came_units, members, span)
        kept.append(own)
    mine = send(jnp.concatenate(kept), lambda p, w: (p - 2 * span * (w // 2), w))
    units = ring_exchange(chunks).reshape(-1, 128)
    far, source = near_product(far_index, far_tiles, far_scale, units)
    near = last_product(near_index, near_tiles, scale, source)
    chip = near + send(far, lambda p, w: (p + span, w))
    last = pair_exchange(chip, pairs).sum(axis=0)
    return finish(core_ref, ordered, root, [mine, last, swap_cores(mine), swap_cores(last)])


def solution(mesh):
    return jax.shard_map(
        local,
        mesh=mesh,
        in_specs=(
            P("blk", None),
            P("blk", "rep", None, None),
            P("blk", "rep"),
            P("blk", "rep"),
            P("blk"),
            P("blk"),
        ),
        out_specs=P(None, "blk", None),
        check_vma=False,
    )
```

```python
import functools

import jax
import jax.numpy as jnp
from jax import lax
from jax.experimental import pallas as pl
from jax.experimental.pallas import tpu as pltpu
from jax.sharding import PartitionSpec as P

HOPS = 4
HALF = 64
VMEM_BYTES = 16 * 2**20


def send(block, place):
    cycle, groups = lax.axis_size("blk"), lax.axis_size("rep")
    route = []
    for p in range(cycle):
        for w in range(groups):
            to_p, to_w = place(p, w)
            route.append((p * groups + w, (to_p % cycle) * groups + to_w))
    return lax.ppermute(block, ("blk", "rep"), route)


def swap_cores(block):
    return send(block, lambda p, w: (p, w ^ 1))


def turned(field):
    return field.reshape(-1, 128, 128).transpose(0, 2, 1)


def split_tiles(rows, first_slots, second_slots, core_ref, mine_ref, other_ref, out_ref):
    def read(i, at, slots):
        held, place = at
        ref = mine_ref if held == "mine" else other_ref
        per_row = 1 + max(p for _, p in slots)
        first = (i * per_row + place) * 128
        return ref[first:first + 128]

    for i in range(rows):
        for s, (at_first, at_second) in enumerate(zip(first_slots, second_slots)):
            tile = jnp.where(core_ref[0] == 0, read(i, at_first, first_slots), read(i, at_second, second_slots)).T
            high = tile.astype(jnp.bfloat16)
            low = (tile - high.astype(jnp.float32)).astype(jnp.bfloat16)
            out_ref[i, s * 128:(s + 1) * 128, 0:128] = high
            out_ref[i, s * 128:(s + 1) * 128, 128:256] = low


def tile_parts(core, mine, other, rows, first_slots, second_slots):
    vmem = pl.BlockSpec(memory_space=pltpu.VMEM)
    return pl.pallas_call(
        functools.partial(split_tiles, rows, first_slots, second_slots),
        in_specs=[pl.BlockSpec(memory_space=pltpu.SMEM), vmem, vmem],
        out_specs=vmem,
        out_shape=jax.ShapeDtypeStruct((rows, len(first_slots) * 128, 256), jnp.bfloat16),
        compiler_params=pltpu.CompilerParams(vmem_limit_bytes=VMEM_BYTES),
    )(core, mine, other)


def multiply(index_ref, tiles_ref, scale_ref, source_ref, gathered_ref, out_ref):
    rows, slots = index_ref.shape
    for i in range(rows):
        for s in range(slots):
            gathered_ref[i, :, s * 128:(s + 1) * 128] = source_ref[index_ref[i, s]]
    for i in range(rows):
        both = jnp.dot(gathered_ref[i], tiles_ref[i], preferred_element_type=jnp.float32)
        total = both[0:HALF] + both[HALF:128]
        out_ref[i * HALF:(i + 1) * HALF] = (total[:, 0:128] + total[:, 128:256]) * scale_ref[i:i + 1]


def near_kernel(index_ref, tiles_ref, scale_ref, units_ref, near_ref, source_ref, gathered_ref):
    count = units_ref.shape[0] // HALF
    for k in range(count):
        part = units_ref[k * HALF:(k + 1) * HALF]
        high = part.astype(jnp.bfloat16)
        source_ref[k, 0:HALF] = high
        source_ref[k, HALF:128] = (part - high.astype(jnp.float32)).astype(jnp.bfloat16)
    source_ref[count] = jnp.zeros((128, 128), jnp.bfloat16)
    multiply(index_ref, tiles_ref, scale_ref, source_ref, gathered_ref, near_ref)


def last_kernel(index_ref, tiles_ref, scale_ref, source_ref, out_ref, gathered_ref):
    multiply(index_ref, tiles_ref, scale_ref, source_ref, gathered_ref, out_ref)


def far_kernel(members, index_ref, tiles_ref, scale_ref, source_ref, near_ref, out_ref, gathered_ref, far_ref):
    multiply(index_ref, tiles_ref, scale_ref, source_ref, gathered_ref, far_ref)
    piece = near_ref.shape[0] // members
    for m in range(members):
        at = slice(m * piece, (m + 1) * piece)
        out_ref[2 * m * piece:(2 * m + 1) * piece] = near_ref[at]
        out_ref[(2 * m + 1) * piece:(2 * m + 2) * piece] = far_ref[at]


def product_call(kernel, inputs, rows, slots, out_shape, more_scratch=()):
    vmem = pl.BlockSpec(memory_space=pltpu.VMEM)
    smem = pl.BlockSpec(memory_space=pltpu.SMEM)
    return pl.pallas_call(
        kernel,
        in_specs=[smem] + [vmem] * (inputs - 1),
        out_specs=jax.tree.map(lambda _: vmem, out_shape),
        out_shape=out_shape,
        scratch_shapes=[pltpu.VMEM((rows, 128, slots * 128), jnp.bfloat16), *more_scratch],
        compiler_params=pltpu.CompilerParams(vmem_limit_bytes=VMEM_BYTES),
        cost_estimate=pl.CostEstimate(flops=2 * rows * slots * 256 * 128 * 128, bytes_accessed=4 * 2**20, transcendentals=0),
    )


def near_product(index, tiles, scale, units):
    rows, slots = index.shape
    sums = jax.ShapeDtypeStruct((rows * HALF, 128), jnp.float32)
    source = jax.ShapeDtypeStruct((units.shape[0] // HALF + 1, 128, 128), jnp.bfloat16)
    return product_call(near_kernel, 4, rows, slots, [sums, source])(index, tiles, scale, units)


def far_product(index, tiles, scale, source, near, members):
    rows, slots = index.shape
    both = jax.ShapeDtypeStruct((2 * rows * HALF, 128), jnp.float32)
    scratch = [pltpu.VMEM((rows * HALF, 128), jnp.float32)]
    return product_call(functools.partial(far_kernel, members), 5, rows, slots, both, scratch)(index, tiles, scale, source, near)


def last_product(index, tiles, scale, source):
    rows, slots = index.shape
    sums = jax.ShapeDtypeStruct((rows * HALF, 128), jnp.float32)
    return product_call(last_kernel, 4, rows, slots, sums)(index, tiles, scale, source)


def piece_sums(came_ref, lines, pairs):
    piece = came_ref.shape[0] // (2 * lines * pairs)

    def read(line, pair, which):
        first = (2 * (line * pairs + pair) + which) * piece
        return came_ref[first:first + piece]

    sums = []
    for line in range(lines):
        terms = [read(line, pair, 0) for pair in range(pairs)]
        terms += [read((line - 1) % lines, pair, 1) for pair in range(pairs)]
        while len(terms) > 1:
            terms = [a + b for a, b in zip(terms[::2], terms[1::2])]
        sums.append(terms[0])
    return sums


def hand_on_kernel(lines, pairs, came_ref, out_ref):
    sums = piece_sums(came_ref, lines, pairs)
    piece = sums[0].shape[0]
    for line in range(lines):
        for pair in range(pairs):
            first = 2 * (line * pairs + pair) * piece
            out_ref[first:first + piece] = sums[(line - 2 * pair) % lines]
            out_ref[first + piece:first + 2 * piece] = sums[(line - 2 * pair - 1) % lines]


def hand_on(came, lines, pairs):
    vmem = pl.BlockSpec(memory_space=pltpu.VMEM)
    return pl.pallas_call(
        functools.partial(hand_on_kernel, lines, pairs),
        in_specs=[vmem],
        out_specs=vmem,
        out_shape=jax.ShapeDtypeStruct(came.shape, jnp.float32),
        compiler_params=pltpu.CompilerParams(vmem_limit_bytes=VMEM_BYTES),
    )(came)


def choose_kernel(members, span, rank_ref, came_ref, chunks_ref, own_ref, behind_ref):
    piece = came_ref.shape[0] // (2 * members)
    for m in range(members):
        at = slice(m * piece, (m + 1) * piece)
        own_ref[at] = came_ref[2 * m * piece:(2 * m + 1) * piece]
        behind_ref[at] = came_ref[(2 * m + 1) * piece:(2 * m + 2) * piece]
    for y in range(span):
        chunks_ref[y] = jnp.where(y >= rank_ref[0], own_ref[...], behind_ref[...])


def choose(rank_y, came, members, span):
    vmem = pl.BlockSpec(memory_space=pltpu.VMEM)
    unit = (came.shape[0] // 2, came.shape[1])
    return pl.pallas_call(
        functools.partial(choose_kernel, members, span),
        in_specs=[pl.BlockSpec(memory_space=pltpu.SMEM), vmem],
        out_specs=[vmem, vmem],
        out_shape=[jax.ShapeDtypeStruct((span, *unit), jnp.float32), jax.ShapeDtypeStruct(unit, jnp.float32)],
        scratch_shapes=[pltpu.VMEM(unit, jnp.float32)],
        compiler_params=pltpu.CompilerParams(vmem_limit_bytes=VMEM_BYTES),
    )(rank_y, came)


def finish_kernel(core_ref, ordered_ref, root_ref, mine_ref, mine_last_ref, other_ref, other_last_ref, out_ref):
    out_ref[0] = ordered_ref[...]
    first_core = core_ref[0] == 0
    blocks = ordered_ref.shape[0] // 128
    size = blocks * HALF
    for hop in range(HOPS):
        for b in range(blocks):
            at = b * HALF if hop == HOPS - 1 else hop * size + b * HALF
            mine = (mine_last_ref if hop == HOPS - 1 else mine_ref)[at:at + HALF]
            other = (other_last_ref if hop == HOPS - 1 else other_ref)[at:at + HALF]
            columns = jnp.concatenate([jnp.where(first_core, mine, other), jnp.where(first_core, other, mine)])
            out_ref[hop + 1, b * 128:(b + 1) * 128] = (columns * root_ref[b:b + 1]).T


def finish(core, ordered, root, fields):
    vmem = pl.BlockSpec(memory_space=pltpu.VMEM)
    return pl.pallas_call(
        finish_kernel,
        in_specs=[pl.BlockSpec(memory_space=pltpu.SMEM)] + [vmem] * (2 + len(fields)),
        out_specs=vmem,
        out_shape=jax.ShapeDtypeStruct((HOPS + 1,) + ordered.shape, jnp.float32),
        compiler_params=pltpu.CompilerParams(vmem_limit_bytes=VMEM_BYTES),
    )(core, ordered, root, *fields)


def ring_exchange(chunks):
    span = chunks.shape[0]
    rings = [[first + at for at in range(span)] for first in range(0, lax.axis_size("blk"), span)]
    return lax.all_to_all(chunks, "blk", 0, 0, axis_index_groups=rings)


def pair_exchange(block, pairs):
    cycle, groups = lax.axis_size("blk"), lax.axis_size("rep")
    sets = [[p * groups + w for w in range(core, groups, 2)] for p in range(cycle) for core in range(2)]
    copies = jnp.broadcast_to(block[None], (pairs, *block.shape))
    return lax.all_to_all(copies, ("blk", "rep"), 0, 0, axis_index_groups=sets)


def plane_exchange(block, span):
    cycle, groups = lax.axis_size("blk"), lax.axis_size("rep")
    planes = [
        [p * groups + w for p in range(y, cycle, span) for w in range(core, groups, 2)]
        for y in range(span) for core in range(2)
    ]
    pieces = block.reshape(len(planes[0]), 1, -1)
    moved = lax.all_to_all(pieces, ("blk", "rep"), 0, 0, axis_index_groups=planes)
    return moved.reshape(block.shape)


def local(features, tile_values, tile_cols, tile_counts, degrees, curve_order):
    rank_blk = lax.axis_index("blk")
    rank_rep = lax.axis_index("rep")
    span = lax.axis_size("blk") // lax.axis_size("rep")
    rows, slots = tile_values.shape[:2]
    mid = slots // 2
    core = rank_rep % 2
    first_core = core == 0
    core_ref = core.reshape(1)

    swapped = swap_cores(tile_values)
    live = jnp.arange(slots, dtype=jnp.int32)[None, :] < tile_counts
    index = jnp.where(live, tile_cols % (span * rows), span * rows)
    swapped_index = swap_cores(index)
    near_index = jnp.where(first_core, index, swapped_index)
    leaving = jnp.where(first_core, swapped[:, :mid], tile_values[:, mid:]).reshape(-1, 128)

    ordered = jnp.take(features, curve_order - rank_blk * features.shape[0], axis=0, mode="clip")
    count = degrees.astype(jnp.float32).reshape(rows, 128)
    inv_root = lax.rsqrt(count)
    root = count * inv_root
    scale = inv_root * inv_root
    sent = turned(ordered) * inv_root[:, None]
    start = jnp.where(first_core, sent[:, :HALF], sent[:, HALF:]).reshape(-1, 128)

    def aligned(p, w):
        return p + 2 * span * (w // 2), w

    def behind_aligned(p, w):
        return p + 2 * span * (w // 2) + span, w

    rank_y = rank_blk % span
    lines = lax.axis_size("blk") // span
    pairs = lax.axis_size("rep") // 2
    members = lines * pairs
    own, behind = send(start, aligned), send(start, behind_aligned)
    leaving_index = jnp.where(first_core, swapped_index, index).astype(jnp.float32)
    far_rows = jnp.concatenate([scale, jnp.pad(leaving_index, ((0, 0), (0, 128 - slots)))])
    own, behind, leaving = lax.optimization_barrier((own, behind, leaving))
    came = send(leaving, lambda p, w: (p - span, w))
    every = [("mine", s) for s in range(slots)], [("other", s) for s in range(slots)]
    flat = tile_values.reshape(-1, 128), swapped.reshape(-1, 128)
    near_tiles = tile_parts(core_ref, *flat, rows, *every)
    near_tiles, far_rows = lax.optimization_barrier((near_tiles, far_rows))
    far_parts = send(far_rows, lambda p, w: (p - span, w))
    ring = jnp.arange(span, dtype=jnp.int32)[:, None, None]
    chunks = jnp.where(ring >= rank_y, own[None], behind[None])
    kept = []
    for hop in range(HOPS - 1):
        units = ring_exchange(chunks).reshape(-1, 128)
        if hop == 0:
            came, near_tiles, far_parts = lax.optimization_barrier((came, near_tiles, far_parts))
            far_scale = far_parts[:rows]
            far_index = far_parts[rows:, :slots].astype(jnp.int32)
        near, source = near_product(near_index, near_tiles, scale, units)
        if hop == 0:
            rest = swap_cores(came)
            low_slots = [("mine", s) for s in range(mid)] + [("other", s) for s in range(mid)]
            high_slots = [("other", s) for s in range(mid)] + [("mine", s) for s in range(mid)]
            far_tiles = tile_parts(core_ref, came, rest, rows, low_slots, high_slots)
        sums = far_product(far_index, far_tiles, far_scale, source, near, members)
        pieces = plane_exchange(sums, span)
        came_units = plane_exchange(hand_on(pieces, lines, pairs), span)
        chunks, own = choose(rank_y.reshape(1), came_units, members, span)
        kept.append(own)
    mine = send(jnp.concatenate(kept), lambda p, w: (p - 2 * span * (w // 2), w))
    units = ring_exchange(chunks).reshape(-1, 128)
    far, source = near_product(far_index, far_tiles, far_scale, units)
    near = last_product(near_index, near_tiles, scale, source)
    chip = near + send(far, lambda p, w: (p + span, w))
    last = pair_exchange(chip, pairs).sum(axis=0)
    return finish(core_ref, ordered, root, [mine, last, swap_cores(mine), swap_cores(last)])


def solution(mesh):
    return jax.shard_map(
        local,
        mesh=mesh,
        in_specs=(
            P("blk", None),
            P("blk", "rep", None, None),
            P("blk", "rep"),
            P("blk", "rep"),
            P("blk"),
            P("blk"),
        ),
        out_specs=P(None, "blk", None),
        check_vma=False,
    )
```

```python
import functools

import jax
import jax.numpy as jnp
from jax import lax
from jax.experimental import pallas as pl
from jax.experimental.pallas import tpu as pltpu
from jax.sharding import PartitionSpec as P

HOPS = 4
HALF = 64
VMEM_BYTES = 16 * 2**20


def send(block, place):
    cycle, groups = lax.axis_size("blk"), lax.axis_size("rep")
    route = []
    for p in range(cycle):
        for w in range(groups):
            to_p, to_w = place(p, w)
            route.append((p * groups + w, (to_p % cycle) * groups + to_w))
    return lax.ppermute(block, ("blk", "rep"), route)


def swap_cores(block):
    return send(block, lambda p, w: (p, w ^ 1))


def turned(field):
    return field.reshape(-1, 128, 128).transpose(0, 2, 1)


def split_tiles(rows, first_slots, second_slots, core_ref, mine_ref, other_ref, out_ref):
    def read(i, at, slots):
        held, place = at
        ref = mine_ref if held == "mine" else other_ref
        per_row = 1 + max(p for _, p in slots)
        first = (i * per_row + place) * 128
        return ref[first:first + 128]

    for i in range(rows):
        for s, (at_first, at_second) in enumerate(zip(first_slots, second_slots)):
            tile = jnp.where(core_ref[0] == 0, read(i, at_first, first_slots), read(i, at_second, second_slots)).T
            high = tile.astype(jnp.bfloat16)
            low = (tile - high.astype(jnp.float32)).astype(jnp.bfloat16)
            out_ref[i, s * 128:(s + 1) * 128, 0:128] = high
            out_ref[i, s * 128:(s + 1) * 128, 128:256] = low


def tile_parts(core, mine, other, rows, first_slots, second_slots):
    vmem = pl.BlockSpec(memory_space=pltpu.VMEM)
    return pl.pallas_call(
        functools.partial(split_tiles, rows, first_slots, second_slots),
        in_specs=[pl.BlockSpec(memory_space=pltpu.SMEM), vmem, vmem],
        out_specs=vmem,
        out_shape=jax.ShapeDtypeStruct((rows, len(first_slots) * 128, 256), jnp.bfloat16),
        compiler_params=pltpu.CompilerParams(vmem_limit_bytes=VMEM_BYTES),
    )(core, mine, other)


def multiply(index_ref, tiles_ref, scale_ref, source_ref, gathered_ref, out_ref):
    rows, slots = index_ref.shape
    for i in range(rows):
        for s in range(slots):
            gathered_ref[i, :, s * 128:(s + 1) * 128] = source_ref[index_ref[i, s]]
    for i in range(rows):
        both = jnp.dot(gathered_ref[i], tiles_ref[i], preferred_element_type=jnp.float32)
        total = both[0:HALF] + both[HALF:128]
        out_ref[i * HALF:(i + 1) * HALF] = (total[:, 0:128] + total[:, 128:256]) * scale_ref[i:i + 1]


def near_kernel(index_ref, tiles_ref, scale_ref, units_ref, near_ref, source_ref, gathered_ref):
    count = units_ref.shape[0] // HALF
    for k in range(count):
        part = units_ref[k * HALF:(k + 1) * HALF]
        high = part.astype(jnp.bfloat16)
        source_ref[k, 0:HALF] = high
        source_ref[k, HALF:128] = (part - high.astype(jnp.float32)).astype(jnp.bfloat16)
    source_ref[count] = jnp.zeros((128, 128), jnp.bfloat16)
    multiply(index_ref, tiles_ref, scale_ref, source_ref, gathered_ref, near_ref)


def last_kernel(index_ref, tiles_ref, scale_ref, source_ref, out_ref, gathered_ref):
    multiply(index_ref, tiles_ref, scale_ref, source_ref, gathered_ref, out_ref)


def far_kernel(members, index_ref, tiles_ref, scale_ref, source_ref, near_ref, out_ref, gathered_ref, far_ref):
    multiply(index_ref, tiles_ref, scale_ref, source_ref, gathered_ref, far_ref)
    piece = near_ref.shape[0] // members
    for m in range(members):
        at = slice(m * piece, (m + 1) * piece)
        out_ref[2 * m * piece:(2 * m + 1) * piece] = near_ref[at]
        out_ref[(2 * m + 1) * piece:(2 * m + 2) * piece] = far_ref[at]


def product_call(kernel, inputs, rows, slots, out_shape, more_scratch=()):
    vmem = pl.BlockSpec(memory_space=pltpu.VMEM)
    smem = pl.BlockSpec(memory_space=pltpu.SMEM)
    return pl.pallas_call(
        kernel,
        in_specs=[smem] + [vmem] * (inputs - 1),
        out_specs=jax.tree.map(lambda _: vmem, out_shape),
        out_shape=out_shape,
        scratch_shapes=[pltpu.VMEM((rows, 128, slots * 128), jnp.bfloat16), *more_scratch],
        compiler_params=pltpu.CompilerParams(vmem_limit_bytes=VMEM_BYTES),
        cost_estimate=pl.CostEstimate(flops=2 * rows * slots * 256 * 128 * 128, bytes_accessed=4 * 2**20, transcendentals=0),
    )


def near_product(index, tiles, scale, units):
    rows, slots = index.shape
    sums = jax.ShapeDtypeStruct((rows * HALF, 128), jnp.float32)
    source = jax.ShapeDtypeStruct((units.shape[0] // HALF + 1, 128, 128), jnp.bfloat16)
    return product_call(near_kernel, 4, rows, slots, [sums, source])(index, tiles, scale, units)


def far_product(index, tiles, scale, source, near, members):
    rows, slots = index.shape
    both = jax.ShapeDtypeStruct((2 * rows * HALF, 128), jnp.float32)
    scratch = [pltpu.VMEM((rows * HALF, 128), jnp.float32)]
    return product_call(functools.partial(far_kernel, members), 5, rows, slots, both, scratch)(index, tiles, scale, source, near)


def last_product(index, tiles, scale, source):
    rows, slots = index.shape
    sums = jax.ShapeDtypeStruct((rows * HALF, 128), jnp.float32)
    return product_call(last_kernel, 4, rows, slots, sums)(index, tiles, scale, source)


def member_of(line, pair, pairs):
    return line // 2 * 2 * pairs + 2 * pair + line % 2


def piece_sums(came_ref, lines, pairs):
    piece = came_ref.shape[0] // (2 * lines * pairs)

    def read(line, pair, which):
        first = (2 * member_of(line, pair, pairs) + which) * piece
        return came_ref[first:first + piece]

    sums = []
    for line in range(lines):
        terms = [read(line, pair, 0) for pair in range(pairs)]
        terms += [read((line - 1) % lines, pair, 1) for pair in range(pairs)]
        while len(terms) > 1:
            terms = [a + b for a, b in zip(terms[::2], terms[1::2])]
        sums.append(terms[0])
    return sums


def hand_on_kernel(lines, pairs, came_ref, out_ref):
    sums = piece_sums(came_ref, lines, pairs)
    piece = sums[0].shape[0]
    for line in range(lines):
        for pair in range(pairs):
            first = 2 * member_of(line, pair, pairs) * piece
            out_ref[first:first + piece] = sums[(line - 2 * pair) % lines]
            out_ref[first + piece:first + 2 * piece] = sums[(line - 2 * pair - 1) % lines]


def hand_on(came, lines, pairs):
    vmem = pl.BlockSpec(memory_space=pltpu.VMEM)
    return pl.pallas_call(
        functools.partial(hand_on_kernel, lines, pairs),
        in_specs=[vmem],
        out_specs=vmem,
        out_shape=jax.ShapeDtypeStruct(came.shape, jnp.float32),
        compiler_params=pltpu.CompilerParams(vmem_limit_bytes=VMEM_BYTES),
    )(came)


def choose_kernel(members, span, rank_ref, came_ref, chunks_ref, own_ref, behind_ref):
    piece = came_ref.shape[0] // (2 * members)
    for m in range(members):
        at = slice(m * piece, (m + 1) * piece)
        own_ref[at] = came_ref[2 * m * piece:(2 * m + 1) * piece]
        behind_ref[at] = came_ref[(2 * m + 1) * piece:(2 * m + 2) * piece]
    for y in range(span):
        chunks_ref[y] = jnp.where(y >= rank_ref[0], own_ref[...], behind_ref[...])


def choose(rank_y, came, members, span):
    vmem = pl.BlockSpec(memory_space=pltpu.VMEM)
    unit = (came.shape[0] // 2, came.shape[1])
    return pl.pallas_call(
        functools.partial(choose_kernel, members, span),
        in_specs=[pl.BlockSpec(memory_space=pltpu.SMEM), vmem],
        out_specs=[vmem, vmem],
        out_shape=[jax.ShapeDtypeStruct((span, *unit), jnp.float32), jax.ShapeDtypeStruct(unit, jnp.float32)],
        scratch_shapes=[pltpu.VMEM(unit, jnp.float32)],
        compiler_params=pltpu.CompilerParams(vmem_limit_bytes=VMEM_BYTES),
    )(rank_y, came)


def finish_kernel(core_ref, ordered_ref, root_ref, mine_ref, mine_last_ref, other_ref, other_last_ref, out_ref):
    out_ref[0] = ordered_ref[...]
    first_core = core_ref[0] == 0
    blocks = ordered_ref.shape[0] // 128
    size = blocks * HALF
    for hop in range(HOPS):
        for b in range(blocks):
            at = b * HALF if hop == HOPS - 1 else hop * size + b * HALF
            mine = (mine_last_ref if hop == HOPS - 1 else mine_ref)[at:at + HALF]
            other = (other_last_ref if hop == HOPS - 1 else other_ref)[at:at + HALF]
            columns = jnp.concatenate([jnp.where(first_core, mine, other), jnp.where(first_core, other, mine)])
            out_ref[hop + 1, b * 128:(b + 1) * 128] = (columns * root_ref[b:b + 1]).T


def finish(core, ordered, root, fields):
    vmem = pl.BlockSpec(memory_space=pltpu.VMEM)
    return pl.pallas_call(
        finish_kernel,
        in_specs=[pl.BlockSpec(memory_space=pltpu.SMEM)] + [vmem] * (2 + len(fields)),
        out_specs=vmem,
        out_shape=jax.ShapeDtypeStruct((HOPS + 1,) + ordered.shape, jnp.float32),
        compiler_params=pltpu.CompilerParams(vmem_limit_bytes=VMEM_BYTES),
    )(core, ordered, root, *fields)


def ring_exchange(chunks):
    span = chunks.shape[0]
    rings = [[first + at for at in range(span)] for first in range(0, lax.axis_size("blk"), span)]
    return lax.all_to_all(chunks, "blk", 0, 0, axis_index_groups=rings)


def copies_kernel(near_ref, far_ref, out_ref):
    total = near_ref[...] + far_ref[...]
    for pair in range(out_ref.shape[0]):
        out_ref[pair] = total


def pair_exchange(near, far, pairs):
    vmem = pl.BlockSpec(memory_space=pltpu.VMEM)
    copies = pl.pallas_call(
        copies_kernel,
        in_specs=[vmem, vmem],
        out_specs=vmem,
        out_shape=jax.ShapeDtypeStruct((pairs, *near.shape), jnp.float32),
        compiler_params=pltpu.CompilerParams(vmem_limit_bytes=VMEM_BYTES),
    )(near, far)
    cycle, groups = lax.axis_size("blk"), lax.axis_size("rep")
    sets = [[p * groups + w for w in range(core, groups, 2)] for p in range(cycle) for core in range(2)]
    return lax.all_to_all(copies, ("blk", "rep"), 0, 0, axis_index_groups=sets)


def plane_exchange(block, span):
    cycle, groups = lax.axis_size("blk"), lax.axis_size("rep")
    pairs = groups // 2
    places = sorted((member_of(line, pair, pairs), line, pair) for line in range(cycle // span) for pair in range(pairs))
    planes = [
        [(line * span + y) * groups + 2 * pair + core for _, line, pair in places]
        for y in range(span) for core in range(2)
    ]
    pieces = block.reshape(len(planes[0]), 1, -1)
    moved = lax.all_to_all(pieces, ("blk", "rep"), 0, 0, axis_index_groups=planes)
    return moved.reshape(block.shape)


def local(features, tile_values, tile_cols, tile_counts, degrees, curve_order):
    rank_blk = lax.axis_index("blk")
    rank_rep = lax.axis_index("rep")
    span = lax.axis_size("blk") // lax.axis_size("rep")
    rows, slots = tile_values.shape[:2]
    mid = slots // 2
    core = rank_rep % 2
    first_core = core == 0
    core_ref = core.reshape(1)

    swapped = swap_cores(tile_values)
    live = jnp.arange(slots, dtype=jnp.int32)[None, :] < tile_counts
    index = jnp.where(live, tile_cols % (span * rows), span * rows)
    swapped_index = swap_cores(index)
    near_index = jnp.where(first_core, index, swapped_index)
    leaving = jnp.where(first_core, swapped[:, :mid], tile_values[:, mid:]).reshape(-1, 128)

    ordered = jnp.take(features, curve_order - rank_blk * features.shape[0], axis=0, mode="clip")
    count = degrees.astype(jnp.float32).reshape(rows, 128)
    inv_root = lax.rsqrt(count)
    root = count * inv_root
    scale = inv_root * inv_root
    sent = turned(ordered) * inv_root[:, None]
    start = jnp.where(first_core, sent[:, :HALF], sent[:, HALF:]).reshape(-1, 128)

    def aligned(p, w):
        return p + 2 * span * (w // 2), w

    def behind_aligned(p, w):
        return p + 2 * span * (w // 2) + span, w

    rank_y = rank_blk % span
    lines = lax.axis_size("blk") // span
    pairs = lax.axis_size("rep") // 2
    members = lines * pairs
    own, behind = send(start, aligned), send(start, behind_aligned)
    leaving_index = jnp.where(first_core, swapped_index, index).astype(jnp.float32)
    far_rows = jnp.concatenate([scale, jnp.pad(leaving_index, ((0, 0), (0, 128 - slots)))])
    own, behind, leaving = lax.optimization_barrier((own, behind, leaving))
    came = send(leaving, lambda p, w: (p - span, w))
    every = [("mine", s) for s in range(slots)], [("other", s) for s in range(slots)]
    flat = tile_values.reshape(-1, 128), swapped.reshape(-1, 128)
    near_tiles = tile_parts(core_ref, *flat, rows, *every)
    near_tiles, far_rows = lax.optimization_barrier((near_tiles, far_rows))
    far_parts = send(far_rows, lambda p, w: (p - span, w))
    ring = jnp.arange(span, dtype=jnp.int32)[:, None, None]
    chunks = jnp.where(ring >= rank_y, own[None], behind[None])
    kept = []
    for hop in range(HOPS - 1):
        units = ring_exchange(chunks).reshape(-1, 128)
        if hop == 0:
            came, near_tiles, far_parts = lax.optimization_barrier((came, near_tiles, far_parts))
            far_scale = far_parts[:rows]
            far_index = far_parts[rows:, :slots].astype(jnp.int32)
        near, source = near_product(near_index, near_tiles, scale, units)
        if hop == 0:
            rest = swap_cores(came)
            low_slots = [("mine", s) for s in range(mid)] + [("other", s) for s in range(mid)]
            high_slots = [("other", s) for s in range(mid)] + [("mine", s) for s in range(mid)]
            far_tiles = tile_parts(core_ref, came, rest, rows, low_slots, high_slots)
        sums = far_product(far_index, far_tiles, far_scale, source, near, members)
        pieces = plane_exchange(sums, span)
        came_units = plane_exchange(hand_on(pieces, lines, pairs), span)
        chunks, own = choose(rank_y.reshape(1), came_units, members, span)
        kept.append(own)
    mine = send(jnp.concatenate(kept), lambda p, w: (p - 2 * span * (w // 2), w))
    units = ring_exchange(chunks).reshape(-1, 128)
    far, source = near_product(far_index, far_tiles, far_scale, units)
    near = last_product(near_index, near_tiles, scale, source)
    last = pair_exchange(near, send(far, lambda p, w: (p + span, w)), pairs).sum(axis=0)
    return finish(core_ref, ordered, root, [mine, last, swap_cores(mine), swap_cores(last)])


def solution(mesh):
    return jax.shard_map(
        local,
        mesh=mesh,
        in_specs=(
            P("blk", None),
            P("blk", "rep", None, None),
            P("blk", "rep"),
            P("blk", "rep"),
            P("blk"),
            P("blk"),
        ),
        out_specs=P(None, "blk", None),
        check_vma=False,
    )
```

```python
import functools

import jax
import jax.numpy as jnp
from jax import lax
from jax.experimental import pallas as pl
from jax.experimental.pallas import tpu as pltpu
from jax.sharding import PartitionSpec as P

HOPS = 4
HALF = 64
VMEM_BYTES = 16 * 2**20


def send(block, place):
    cycle, groups = lax.axis_size("blk"), lax.axis_size("rep")
    route = []
    for p in range(cycle):
        for w in range(groups):
            to_p, to_w = place(p, w)
            route.append((p * groups + w, (to_p % cycle) * groups + to_w))
    return lax.ppermute(block, ("blk", "rep"), route)


def swap_cores(block):
    return send(block, lambda p, w: (p, w ^ 1))


def turned(field):
    return field.reshape(-1, 128, 128).transpose(0, 2, 1)


def split_tiles(rows, first_slots, second_slots, core_ref, mine_ref, other_ref, out_ref):
    def read(i, at, slots):
        held, place = at
        ref = mine_ref if held == "mine" else other_ref
        per_row = 1 + max(p for _, p in slots)
        first = (i * per_row + place) * 128
        return ref[first:first + 128]

    for i in range(rows):
        for s, (at_first, at_second) in enumerate(zip(first_slots, second_slots)):
            tile = jnp.where(core_ref[0] == 0, read(i, at_first, first_slots), read(i, at_second, second_slots)).T
            high = tile.astype(jnp.bfloat16)
            low = (tile - high.astype(jnp.float32)).astype(jnp.bfloat16)
            out_ref[i, s * 128:(s + 1) * 128, 0:128] = high
            out_ref[i, s * 128:(s + 1) * 128, 128:256] = low


def tile_parts(core, mine, other, rows, first_slots, second_slots):
    vmem = pl.BlockSpec(memory_space=pltpu.VMEM)
    return pl.pallas_call(
        functools.partial(split_tiles, rows, first_slots, second_slots),
        in_specs=[pl.BlockSpec(memory_space=pltpu.SMEM), vmem, vmem],
        out_specs=vmem,
        out_shape=jax.ShapeDtypeStruct((rows, len(first_slots) * 128, 256), jnp.bfloat16),
        compiler_params=pltpu.CompilerParams(vmem_limit_bytes=VMEM_BYTES),
    )(core, mine, other)


def multiply(index_ref, tiles_ref, scale_ref, source_ref, gathered_ref, out_ref):
    rows, slots = index_ref.shape
    for i in range(rows):
        for s in range(slots):
            gathered_ref[i, :, s * 128:(s + 1) * 128] = source_ref[index_ref[i, s]]
    for i in range(rows):
        both = jnp.dot(gathered_ref[i], tiles_ref[i], preferred_element_type=jnp.float32)
        total = both[0:HALF] + both[HALF:128]
        out_ref[i * HALF:(i + 1) * HALF] = (total[:, 0:128] + total[:, 128:256]) * scale_ref[i:i + 1]


def near_kernel(index_ref, tiles_ref, scale_ref, units_ref, near_ref, source_ref, gathered_ref):
    count = units_ref.shape[0] // HALF
    for k in range(count):
        part = units_ref[k * HALF:(k + 1) * HALF]
        high = part.astype(jnp.bfloat16)
        source_ref[k, 0:HALF] = high
        source_ref[k, HALF:128] = (part - high.astype(jnp.float32)).astype(jnp.bfloat16)
    source_ref[count] = jnp.zeros((128, 128), jnp.bfloat16)
    multiply(index_ref, tiles_ref, scale_ref, source_ref, gathered_ref, near_ref)


def last_kernel(index_ref, tiles_ref, scale_ref, source_ref, out_ref, gathered_ref):
    multiply(index_ref, tiles_ref, scale_ref, source_ref, gathered_ref, out_ref)


def far_kernel(members, index_ref, tiles_ref, scale_ref, source_ref, near_ref, out_ref, gathered_ref, far_ref):
    multiply(index_ref, tiles_ref, scale_ref, source_ref, gathered_ref, far_ref)
    piece = near_ref.shape[0] // members
    for m in range(members):
        at = slice(m * piece, (m + 1) * piece)
        out_ref[2 * m * piece:(2 * m + 1) * piece] = near_ref[at]
        out_ref[(2 * m + 1) * piece:(2 * m + 2) * piece] = far_ref[at]


def product_call(kernel, inputs, rows, slots, out_shape, more_scratch=()):
    vmem = pl.BlockSpec(memory_space=pltpu.VMEM)
    smem = pl.BlockSpec(memory_space=pltpu.SMEM)
    return pl.pallas_call(
        kernel,
        in_specs=[smem] + [vmem] * (inputs - 1),
        out_specs=jax.tree.map(lambda _: vmem, out_shape),
        out_shape=out_shape,
        scratch_shapes=[pltpu.VMEM((rows, 128, slots * 128), jnp.bfloat16), *more_scratch],
        compiler_params=pltpu.CompilerParams(vmem_limit_bytes=VMEM_BYTES),
        cost_estimate=pl.CostEstimate(flops=2 * rows * slots * 256 * 128 * 128, bytes_accessed=4 * 2**20, transcendentals=0),
    )


def near_product(index, tiles, scale, units):
    rows, slots = index.shape
    sums = jax.ShapeDtypeStruct((rows * HALF, 128), jnp.float32)
    source = jax.ShapeDtypeStruct((units.shape[0] // HALF + 1, 128, 128), jnp.bfloat16)
    return product_call(near_kernel, 4, rows, slots, [sums, source])(index, tiles, scale, units)


def far_product(index, tiles, scale, source, near, members):
    rows, slots = index.shape
    both = jax.ShapeDtypeStruct((2 * rows * HALF, 128), jnp.float32)
    scratch = [pltpu.VMEM((rows * HALF, 128), jnp.float32)]
    return product_call(functools.partial(far_kernel, members), 5, rows, slots, both, scratch)(index, tiles, scale, source, near)


def last_product(index, tiles, scale, source):
    rows, slots = index.shape
    sums = jax.ShapeDtypeStruct((rows * HALF, 128), jnp.float32)
    return product_call(last_kernel, 4, rows, slots, sums)(index, tiles, scale, source)


def member_of(line, pair, pairs):
    return (2 * pair + line % 2) * pairs + line // 2


def piece_sums(came_ref, lines, pairs):
    piece = came_ref.shape[0] // (2 * lines * pairs)

    def read(line, pair, which):
        first = (2 * member_of(line, pair, pairs) + which) * piece
        return came_ref[first:first + piece]

    sums = []
    for line in range(lines):
        terms = [read(line, pair, 0) for pair in range(pairs)]
        terms += [read((line - 1) % lines, pair, 1) for pair in range(pairs)]
        while len(terms) > 1:
            terms = [a + b for a, b in zip(terms[::2], terms[1::2])]
        sums.append(terms[0])
    return sums


def hand_on_kernel(lines, pairs, came_ref, out_ref):
    sums = piece_sums(came_ref, lines, pairs)
    piece = sums[0].shape[0]
    for line in range(lines):
        for pair in range(pairs):
            first = 2 * member_of(line, pair, pairs) * piece
            out_ref[first:first + piece] = sums[(line - 2 * pair) % lines]
            out_ref[first + piece:first + 2 * piece] = sums[(line - 2 * pair - 1) % lines]


def hand_on(came, lines, pairs):
    vmem = pl.BlockSpec(memory_space=pltpu.VMEM)
    return pl.pallas_call(
        functools.partial(hand_on_kernel, lines, pairs),
        in_specs=[vmem],
        out_specs=vmem,
        out_shape=jax.ShapeDtypeStruct(came.shape, jnp.float32),
        compiler_params=pltpu.CompilerParams(vmem_limit_bytes=VMEM_BYTES),
    )(came)


def choose_kernel(members, span, rank_ref, came_ref, chunks_ref, own_ref, behind_ref):
    piece = came_ref.shape[0] // (2 * members)
    for m in range(members):
        at = slice(m * piece, (m + 1) * piece)
        own_ref[at] = came_ref[2 * m * piece:(2 * m + 1) * piece]
        behind_ref[at] = came_ref[(2 * m + 1) * piece:(2 * m + 2) * piece]
    for y in range(span):
        chunks_ref[y] = jnp.where(y >= rank_ref[0], own_ref[...], behind_ref[...])


def choose(rank_y, came, members, span):
    vmem = pl.BlockSpec(memory_space=pltpu.VMEM)
    unit = (came.shape[0] // 2, came.shape[1])
    return pl.pallas_call(
        functools.partial(choose_kernel, members, span),
        in_specs=[pl.BlockSpec(memory_space=pltpu.SMEM), vmem],
        out_specs=[vmem, vmem],
        out_shape=[jax.ShapeDtypeStruct((span, *unit), jnp.float32), jax.ShapeDtypeStruct(unit, jnp.float32)],
        scratch_shapes=[pltpu.VMEM(unit, jnp.float32)],
        compiler_params=pltpu.CompilerParams(vmem_limit_bytes=VMEM_BYTES),
    )(rank_y, came)


def finish_kernel(core_ref, ordered_ref, root_ref, mine_ref, mine_last_ref, other_ref, other_last_ref, out_ref):
    out_ref[0] = ordered_ref[...]
    first_core = core_ref[0] == 0
    blocks = ordered_ref.shape[0] // 128
    size = blocks * HALF
    for hop in range(HOPS):
        for b in range(blocks):
            at = b * HALF if hop == HOPS - 1 else hop * size + b * HALF
            mine = (mine_last_ref if hop == HOPS - 1 else mine_ref)[at:at + HALF]
            other = (other_last_ref if hop == HOPS - 1 else other_ref)[at:at + HALF]
            columns = jnp.concatenate([jnp.where(first_core, mine, other), jnp.where(first_core, other, mine)])
            out_ref[hop + 1, b * 128:(b + 1) * 128] = (columns * root_ref[b:b + 1]).T


def finish(core, ordered, root, fields):
    vmem = pl.BlockSpec(memory_space=pltpu.VMEM)
    return pl.pallas_call(
        finish_kernel,
        in_specs=[pl.BlockSpec(memory_space=pltpu.SMEM)] + [vmem] * (2 + len(fields)),
        out_specs=vmem,
        out_shape=jax.ShapeDtypeStruct((HOPS + 1,) + ordered.shape, jnp.float32),
        compiler_params=pltpu.CompilerParams(vmem_limit_bytes=VMEM_BYTES),
    )(core, ordered, root, *fields)


def ring_exchange(chunks):
    span = chunks.shape[0]
    rings = [[first + at for at in range(span)] for first in range(0, lax.axis_size("blk"), span)]
    return lax.all_to_all(chunks, "blk", 0, 0, axis_index_groups=rings)


def copies_kernel(near_ref, far_ref, out_ref):
    total = near_ref[...] + far_ref[...]
    for pair in range(out_ref.shape[0]):
        out_ref[pair] = total


def pair_exchange(near, far, pairs):
    vmem = pl.BlockSpec(memory_space=pltpu.VMEM)
    copies = pl.pallas_call(
        copies_kernel,
        in_specs=[vmem, vmem],
        out_specs=vmem,
        out_shape=jax.ShapeDtypeStruct((pairs, *near.shape), jnp.float32),
        compiler_params=pltpu.CompilerParams(vmem_limit_bytes=VMEM_BYTES),
    )(near, far)
    cycle, groups = lax.axis_size("blk"), lax.axis_size("rep")
    sets = [[p * groups + w for w in range(core, groups, 2)] for p in range(cycle) for core in range(2)]
    return lax.all_to_all(copies, ("blk", "rep"), 0, 0, axis_index_groups=sets)


def plane_exchange(block, span):
    cycle, groups = lax.axis_size("blk"), lax.axis_size("rep")
    pairs = groups // 2
    places = sorted((member_of(line, pair, pairs), line, pair) for line in range(cycle // span) for pair in range(pairs))
    planes = [
        [(line * span + y) * groups + 2 * pair + core for _, line, pair in places]
        for y in range(span) for core in range(2)
    ]
    pieces = block.reshape(len(planes[0]), 1, -1)
    moved = lax.all_to_all(pieces, ("blk", "rep"), 0, 0, axis_index_groups=planes)
    return moved.reshape(block.shape)


def local(features, tile_values, tile_cols, tile_counts, degrees, curve_order):
    rank_blk = lax.axis_index("blk")
    rank_rep = lax.axis_index("rep")
    span = lax.axis_size("blk") // lax.axis_size("rep")
    rows, slots = tile_values.shape[:2]
    mid = slots // 2
    core = rank_rep % 2
    first_core = core == 0
    core_ref = core.reshape(1)

    swapped = swap_cores(tile_values)
    live = jnp.arange(slots, dtype=jnp.int32)[None, :] < tile_counts
    index = jnp.where(live, tile_cols % (span * rows), span * rows)
    swapped_index = swap_cores(index)
    near_index = jnp.where(first_core, index, swapped_index)
    leaving = jnp.where(first_core, swapped[:, :mid], tile_values[:, mid:]).reshape(-1, 128)

    ordered = jnp.take(features, curve_order - rank_blk * features.shape[0], axis=0, mode="clip")
    count = degrees.astype(jnp.float32).reshape(rows, 128)
    inv_root = lax.rsqrt(count)
    root = count * inv_root
    scale = inv_root * inv_root
    sent = turned(ordered) * inv_root[:, None]
    start = jnp.where(first_core, sent[:, :HALF], sent[:, HALF:]).reshape(-1, 128)

    def aligned(p, w):
        return p + 2 * span * (w // 2), w

    def behind_aligned(p, w):
        return p + 2 * span * (w // 2) + span, w

    rank_y = rank_blk % span
    lines = lax.axis_size("blk") // span
    pairs = lax.axis_size("rep") // 2
    members = lines * pairs
    own, behind = send(start, aligned), send(start, behind_aligned)
    leaving_index = jnp.where(first_core, swapped_index, index).astype(jnp.float32)
    far_rows = jnp.concatenate([scale, jnp.pad(leaving_index, ((0, 0), (0, 128 - slots)))])
    own, behind, leaving = lax.optimization_barrier((own, behind, leaving))
    came = send(leaving, lambda p, w: (p - span, w))
    every = [("mine", s) for s in range(slots)], [("other", s) for s in range(slots)]
    flat = tile_values.reshape(-1, 128), swapped.reshape(-1, 128)
    near_tiles = tile_parts(core_ref, *flat, rows, *every)
    near_tiles, far_rows = lax.optimization_barrier((near_tiles, far_rows))
    far_parts = send(far_rows, lambda p, w: (p - span, w))
    ring = jnp.arange(span, dtype=jnp.int32)[:, None, None]
    chunks = jnp.where(ring >= rank_y, own[None], behind[None])
    kept = []
    for hop in range(HOPS - 1):
        units = ring_exchange(chunks).reshape(-1, 128)
        if hop == 0:
            came, near_tiles, far_parts = lax.optimization_barrier((came, near_tiles, far_parts))
            far_scale = far_parts[:rows]
            far_index = far_parts[rows:, :slots].astype(jnp.int32)
        near, source = near_product(near_index, near_tiles, scale, units)
        if hop == 0:
            rest = swap_cores(came)
            low_slots = [("mine", s) for s in range(mid)] + [("other", s) for s in range(mid)]
            high_slots = [("other", s) for s in range(mid)] + [("mine", s) for s in range(mid)]
            far_tiles = tile_parts(core_ref, came, rest, rows, low_slots, high_slots)
        sums = far_product(far_index, far_tiles, far_scale, source, near, members)
        pieces = plane_exchange(sums, span)
        came_units = plane_exchange(hand_on(pieces, lines, pairs), span)
        chunks, own = choose(rank_y.reshape(1), came_units, members, span)
        kept.append(own)
    mine = send(jnp.concatenate(kept), lambda p, w: (p - 2 * span * (w // 2), w))
    units = ring_exchange(chunks).reshape(-1, 128)
    far, source = near_product(far_index, far_tiles, far_scale, units)
    near = last_product(near_index, near_tiles, scale, source)
    last = pair_exchange(near, send(far, lambda p, w: (p + span, w)), pairs).sum(axis=0)
    return finish(core_ref, ordered, root, [mine, last, swap_cores(mine), swap_cores(last)])


def solution(mesh):
    return jax.shard_map(
        local,
        mesh=mesh,
        in_specs=(
            P("blk", None),
            P("blk", "rep", None, None),
            P("blk", "rep"),
            P("blk", "rep"),
            P("blk"),
            P("blk"),
        ),
        out_specs=P(None, "blk", None),
        check_vma=False,
    )
```
